1024 devices in a mesh: group: 8 (over z), member: 128 (over y, x, core).
Axes of the slice: x: 8, y: 8, z: 8, core: 2. Of those that a mesh axis runs over, the one named last changes fastest.
Arguments:
- tokens: bfloat16 [1024, 3584], P(('group', 'member')), may hold values from -6 to 6
- grad_out: bfloat16 [1024, 3584], P(('group', 'member')), may hold values from -6 to 6
- route_token: int32 [8, 8, 8, 16], P('group'), may hold values from 0 to 127, as said below
- route_count: int32 [8, 8, 8], P('group'), may hold values from 0 to 16, as said below
- route_prob: float32 [8, 8, 8, 16], P('group'), may hold values from 0.05 to 0.6
- w_gate: bfloat16 [1024, 64, 3584], P(('group', 'member')), may hold values from -0.09375 to 0.09375
- w_up: bfloat16 [1024, 64, 3584], P(('group', 'member')), may hold values from -0.09375 to 0.09375
- w_down: bfloat16 [1024, 64, 3584], P(('group', 'member')), may hold values from -0.1875 to 0.1875
Outputs:
- grad_tokens: bfloat16 [1024, 3584], P(('group', 'member'))
- grad_gate: bfloat16 [1024, 64, 3584], P(('group', 'member'))
- grad_up: bfloat16 [1024, 64, 3584], P(('group', 'member'))
- grad_down: bfloat16 [1024, 64, 3584], P(('group', 'member'))
The draws below stay inside these ranges and needn't reach their ends.
Inputs may be any that keep to these rules, and one draw needn't show every extreme that they name: Each token of a source group is routed to 2 different experts in each of 4 different groups. An expert keeps, for each source group, the first 16 of the tokens routed to it in token order and drops the rest; route_token lists the kept tokens in that order, all different, and slots at or past route_count hold 0. In every draw one expert keeps 16 tokens from every source group. `route_count`: the number of kept tokens of each source group for each expert; 16 is reached in every draw.
All inputs are finite; a program needn't handle non-finite values.
Results may differ from the reference program's by a relative error of at most 0.0058.
Values may be sent and summed in bfloat16 or wider, within the bound.
A program may use at most 32 MiB of HBM per device.

```python
import math
import jax
import jax.numpy as jnp
from jax import lax

D = 3584
FFN = 1024
SPLIT = 16
HS = 64
EPG = 8
SLICES = 1024
LIMIT = 4
PER_GROUP = 2
TOK_GROUP = 128
TOKENS = 1024
CAP = 16
N_GROUP = 8


def routing_tables(key):
    key_groups, key_experts, key_hot_group, key_hot_expert = jax.random.split(key, 4)
    hot_group = jax.random.randint(key_hot_group, (), 0, N_GROUP)
    hot_expert = jax.random.randint(key_hot_expert, (), 0, EPG)
    forced = (jnp.arange(TOK_GROUP, dtype=jnp.int32) < CAP)[None, :]
    group_scores = jax.random.randint(key_groups, (N_GROUP, TOK_GROUP, N_GROUP), 0, 1 << 20)
    group_scores = group_scores * N_GROUP + jnp.arange(N_GROUP, dtype=jnp.int32)
    group_hot = (jnp.arange(N_GROUP, dtype=jnp.int32) == hot_group)[None, None, :]
    group_scores = jnp.where(forced[:, :, None] & group_hot, -1, group_scores)
    group_rank = jnp.argsort(jnp.argsort(group_scores, axis=-1), axis=-1)
    chosen_group = group_rank < LIMIT
    expert_scores = jax.random.randint(key_experts, (N_GROUP, TOK_GROUP, N_GROUP, EPG), 0, 1 << 20)
    expert_scores = expert_scores * EPG + jnp.arange(EPG, dtype=jnp.int32)
    expert_hot = (jnp.arange(EPG, dtype=jnp.int32) == hot_expert)[None, None, None, :]
    expert_scores = jnp.where(forced[:, :, None, None] & group_hot[:, :, :, None] & expert_hot, -1, expert_scores)
    expert_rank = jnp.argsort(jnp.argsort(expert_scores, axis=-1), axis=-1)
    chosen = ((expert_rank < PER_GROUP) & chosen_group[:, :, :, None]).astype(jnp.int32)
    position = jnp.cumsum(chosen, axis=1) - 1
    kept = (chosen > 0) & (position < CAP)
    counts = jnp.minimum(jnp.sum(chosen, axis=1), CAP).astype(jnp.int32)
    slot_match = kept[..., None] & (position[..., None] == jnp.arange(CAP, dtype=jnp.int32))
    token_numbers = jnp.arange(TOK_GROUP, dtype=jnp.int32)[None, :, None, None, None]
    table = jnp.sum(jnp.where(slot_match, token_numbers, 0), axis=1).astype(jnp.int32)
    return (table, counts)


def draw_route_token(key, part):
    tables = routing_tables(key)
    return tables[0]


def draw_route_count(key, part):
    tables = routing_tables(key)
    return tables[1]


def level_of(own_key, shape, cuts, least, largest):
    def one(dim, blocks):
        steps = jax.random.uniform(jax.random.fold_in(jax.random.fold_in(own_key, 6), dim), (blocks,), jnp.float32, least / len(cuts), largest / len(cuts))
        return jnp.repeat(jnp.exp(steps), shape[dim] // blocks).reshape((-1,) + (1,) * (len(shape) - dim - 1))

    factor_of = one(*cuts[0])
    for cut in cuts[1:]:
        factor_of = factor_of * one(*cut)
    return factor_of


def normal_values(stream_key, extent, deviation, limit, cuts=(), held_as=jnp.bfloat16):
    gain = level_of(stream_key, extent, cuts, -0.22, 0.18) if cuts else 1.0
    drawn = jax.random.normal(stream_key, extent, jnp.float32) * deviation * gain
    return jnp.minimum(jnp.maximum(drawn, -limit), limit).astype(held_as)


def setup_inputs(seed: int = 0) -> dict:
    keys = jax.random.split(jax.random.key(seed), 9)
    return {
        "tokens": normal_values(keys[0], (TOKENS, D), 1.0, 6.0, ((0, 1024),)),
        "grad_out": normal_values(keys[1], (TOKENS, D), 1.0, 6.0, ((0, 1024),)),
        "route_token": draw_route_token(jax.random.fold_in(keys[8], 71), 0),
        "route_count": draw_route_count(jax.random.fold_in(keys[8], 71), 0),
        "route_prob": jnp.clip(jnp.exp(math.log(0.6) - 2.4849067 * jax.random.uniform(keys[4], (N_GROUP, N_GROUP, EPG, CAP), jnp.float32) ** level_of(keys[4], (N_GROUP, N_GROUP, EPG, CAP), ((0, 8),), -0.2, 0.2)), 0.05, 0.6),
        "w_gate": normal_values(keys[5], (SLICES, HS, D), D ** -0.5, 0.09375, ((0, 1024),)),
        "w_up": normal_values(keys[6], (SLICES, HS, D), D ** -0.5, 0.09375, ((0, 1024),)),
        "w_down": normal_values(keys[7], (SLICES, HS, D), FFN ** -0.5, 0.1875, ((0, 1024),)),
    }


def slice_backward(rows_x, rows_scaled, gate_weight, up_weight, down_weight):
    gate_value = jnp.dot(rows_x, gate_weight.T, preferred_element_type=jnp.float32)
    up_value = jnp.dot(rows_x, up_weight.T, preferred_element_type=jnp.float32)
    sigma_gate = jax.nn.sigmoid(gate_value)
    active = gate_value * sigma_gate
    hidden = (active * up_value).astype(jnp.bfloat16)
    d_hidden = jnp.dot(rows_scaled, down_weight.T, preferred_element_type=jnp.float32)
    d_gate = (d_hidden * up_value * sigma_gate * (1.0 + gate_value * (1.0 - sigma_gate))).astype(jnp.bfloat16)
    d_up = (d_hidden * active).astype(jnp.bfloat16)
    grad_down = jnp.dot(hidden.T, rows_scaled, preferred_element_type=jnp.float32).astype(jnp.bfloat16)
    grad_gate = jnp.dot(d_gate.T, rows_x, preferred_element_type=jnp.float32).astype(jnp.bfloat16)
    grad_up = jnp.dot(d_up.T, rows_x, preferred_element_type=jnp.float32).astype(jnp.bfloat16)
    partial_rows = jnp.dot(d_gate, gate_weight, preferred_element_type=jnp.float32)
    partial_rows = partial_rows + jnp.dot(d_up, up_weight, preferred_element_type=jnp.float32)
    return grad_gate, grad_up, grad_down, partial_rows


def reference(tokens, grad_out, route_token, route_count, route_prob, w_gate, w_up, w_down):
    source_base = jnp.arange(N_GROUP, dtype=jnp.int32)[:, None] * TOK_GROUP
    slot_index = jnp.arange(CAP, dtype=jnp.int32)[None, :]

    def step_fn(running, inputs):
        gate_weight, up_weight, down_weight, slice_id = inputs
        expert_id = slice_id // SPLIT
        dest_group = expert_id // EPG
        local_expert = expert_id % EPG
        slot_tokens = route_token[:, dest_group, local_expert, :].astype(jnp.int32)
        slot_counts = route_count[:, dest_group, local_expert].astype(jnp.int32)
        live = (slot_index < slot_counts[:, None]).astype(jnp.float32)
        slot_weights = (route_prob[:, dest_group, local_expert, :] * live).reshape(-1)
        global_rows = (source_base + slot_tokens).reshape(-1).astype(jnp.int32)
        rows_x = tokens[global_rows]
        rows_scaled = (slot_weights[:, None] * grad_out[global_rows].astype(jnp.float32)).astype(jnp.bfloat16)
        grad_gate, grad_up, grad_down, partial_rows = slice_backward(rows_x, rows_scaled, gate_weight, up_weight, down_weight)
        running = running.at[global_rows].add(partial_rows)
        return running, (grad_gate, grad_up, grad_down)

    zero_grad = jnp.zeros((TOKENS, D), jnp.float32)
    slice_ids = jnp.arange(SLICES, dtype=jnp.int32)
    summed, outputs = lax.scan(step_fn, zero_grad, (w_gate, w_up, w_down, slice_ids))
    return summed.astype(jnp.bfloat16), outputs[0], outputs[1], outputs[2]
```

```python
import functools

import jax
import jax.numpy as jnp
from jax import lax
from jax.experimental import pallas as pl
from jax.experimental.pallas import tpu as pltpu
from jax.sharding import PartitionSpec as P

MESH = pl.DeviceIdType.MESH
CW = 256
F32 = jnp.float32
BF16 = jnp.bfloat16


def dot_nn(a, b):
    return jnp.dot(a, b, preferred_element_type=F32)


def dot_nt(a, b):
    return lax.dot_general(a, b, (((1,), (1,)), ((), ())), preferred_element_type=F32)


def kernel(
    dims,
    x_ref, dy_ref, tok_ref, cnt_ref, prob_ref, wg, wu, wd,
    gt_ref, gg, gu, gd,
    send_a, recv_a, t_all, z_send, rows, w_gu, w_dd, w_sib, acc_gu, acc_dh,
    sel_t, d_pair, d_t, h_t, p_buf, snd, rcv, r2_send, r2_recv, r3_send, r3_recv,
    r4_send, r4_recv, grads,
    w_sem, out_sem, small_send, small_recv, ring_send, ring_recv, sib_send, sib_recv,
    red_send, red_recv,
):
    ng, ny, nx, hs, cap = dims
    nk = 2 * nx
    nc = nk - 2
    nd = nc // 2
    ns = ng * cap
    tg = ny * nk
    half = ns // 2
    far = nx // 2

    z = lax.axis_index("group")
    m = lax.axis_index("member")
    y = m // nk
    k = m % nk
    x = k // 2
    c = k % 2
    sibling = (z, y * nk + 2 * x + (1 - c))
    neighbour = (
        (z, y * nk + 2 * ((x + 1) % nx) + c),
        (z, y * nk + 2 * ((x + nx - 1) % nx) + c),
    )
    reach = ((far, nx - 1 - far), (nx - 1 - far, far))
    routes = k < nc

    def remote(src, dst, send_sem, recv_sem, device):
        return pltpu.make_async_remote_copy(
            src_ref=src, dst_ref=dst, send_sem=send_sem, recv_sem=recv_sem,
            device_id=device, device_id_type=MESH,
        )

    def arrived(ref, sem):
        pltpu.make_async_copy(ref, ref, sem).wait()

    def signal(device):
        pl.semaphore_signal(
            pltpu.get_barrier_semaphore(), inc=1, device_id=device, device_id_type=MESH
        )

    A, B, C, W, X, R2, R3, R4 = range(8)

    loads = [
        pltpu.make_async_copy(wg.at[0], w_gu.at[pl.ds(0, hs)], w_sem.at[0]),
        pltpu.make_async_copy(wu.at[0], w_gu.at[pl.ds(hs, hs)], w_sem.at[1]),
        pltpu.make_async_copy(wd.at[0], w_dd.at[pl.ds(0, hs)], w_sem.at[2]),
        pltpu.make_async_copy(wd.at[0], w_dd.at[pl.ds(hs, hs)], w_sem.at[3]),
    ]
    for load in loads:
        load.start()

    for o in range(1, nk):
        signal((z, y * nk + (k + o) % nk))
    for o in range(1, ny):
        signal((z, ((y + o) % ny) * nk + k))
    for o in range(1, ng):
        signal(((z + o) % ng, m))

    for u in range(2 * nc):
        cols = slice(u * 128, (u + 1) * 128)
        send_a[u // 2, pl.ds(u % 2, 1), :] = x_ref[:, cols].astype(F32)
        send_a[u // 2, pl.ds(2 + u % 2, 1), :] = dy_ref[:, cols].astype(F32)

    pl.semaphore_wait(pltpu.get_barrier_semaphore(), (nk - 1) + (ny - 1) + (ng - 1))

    for o in range(1, nk):
        kk = (k + o) % nk

        @pl.when(kk < nc)
        def _():
            remote(
                send_a.at[kk], recv_a.at[k], small_send.at[A], small_recv.at[A],
                (z, y * nk + kk),
            ).start()

    row = lax.broadcasted_iota(jnp.int32, (ns, cap), 0)
    lane = lax.broadcasted_iota(jnp.int32, (ns, cap), 1)

    def spread(ref):
        wide = jnp.concatenate(
            [
                jnp.broadcast_to(ref[0, i, pl.ds(y, 1), :].astype(F32), (cap, cap))
                for i in range(ng)
            ],
            axis=0,
        )
        return jnp.sum(jnp.where(lane == row % cap, wide, 0.0), axis=1, keepdims=True)

    counts = jnp.concatenate(
        [
            jnp.broadcast_to(cnt_ref[0, pl.ds(i, 1), :].astype(F32), (cap, ny))
            for i in range(ng)
        ],
        axis=0,
    )
    expert = lax.broadcasted_iota(jnp.int32, (ns, ny), 1)
    counts = jnp.sum(jnp.where(expert == y, counts, 0.0), axis=1, keepdims=True)
    slot_token = spread(tok_ref)
    position = (lax.broadcasted_iota(jnp.int32, (ns, 1), 0) % cap).astype(F32)
    live = jnp.where(position < counts, 1.0, 0.0)
    weight = spread(prob_ref) * live
    token = lax.broadcasted_iota(jnp.int32, (ns, tg), 1).astype(F32)
    sel = jnp.where(token == slot_token, 1.0, 0.0)
    sel_t[...] = (sel * live).T.astype(BF16)
    sel = sel.astype(BF16)

    for load in loads:
        load.wait()
    to_sibling = [
        remote(
            w_gu.at[:, pl.ds(pl.multiple_of((2 * i + 1 - c) * CW, CW), CW)], w_sib.at[i],
            small_send.at[W], small_recv.at[W], sibling,
        )
        for i in range(nd)
    ]
    for copy in to_sibling:
        copy.start()

    acc_gu[...] = jnp.zeros_like(acc_gu)
    acc_dh[...] = jnp.zeros_like(acc_dh)

    def block(source, core, h):
        return rows.at[2 * source + core, pl.ds(h * half, half), :]

    @pl.when(routes)
    def _():
        recv_a[k] = send_a[k]
        arrived(recv_a.at[pl.ds(0, nk - 1)], small_recv.at[A])
        t_all[y] = jnp.concatenate([recv_a[:, u, :] for u in range(4)], axis=1).astype(BF16)
        for o in range(1, ny):
            remote(
                t_all.at[y], t_all.at[y], small_send.at[B], small_recv.at[B],
                (z, ((y + o) % ny) * nk + k),
            ).start()
        arrived(t_all.at[pl.ds(0, ny - 1)], small_recv.at[B])
        picked = dot_nn(sel, t_all[...].reshape(tg, 2 * CW))
        z_send[:, :, 0:CW] = picked[:, 0:CW].astype(BF16).reshape(ng, cap, CW)
        z_send[:, :, CW:] = (picked[:, CW:] * weight).astype(BF16).reshape(ng, cap, CW)
        here = pl.ds(pl.multiple_of(z * cap, cap), cap)
        for o in range(1, ng):
            g = (z + o) % ng
            remote(
                z_send.at[g], rows.at[k, here, :], small_send.at[C], small_recv.at[C], (g, m)
            ).start()
        rows[k, here, :] = z_send[z]
        arrived(rows.at[k, pl.ds(0, ns - cap), :], small_recv.at[C])
        for h in range(2):
            for way in range(2):
                if reach[h][way] >= 1:
                    remote(
                        block(x, c, h), block(x, c, h), ring_send.at[way, 0, h],
                        ring_recv.at[way, 1, h], neighbour[way],
                    ).start()
        for h in range(2):
            remote(
                block(x, c, h), block(x, c, h), sib_send.at[0, 0, h], sib_recv.at[0, 0, h],
                sibling,
            ).start()

    def accumulate(source, core):
        chunk = 2 * source + core
        cols = pl.ds(pl.multiple_of(chunk * CW, CW), CW)
        acc_gu[...] += dot_nt(rows[chunk, :, 0:CW], w_gu[:, cols])
        acc_dh[...] += dot_nt(rows[chunk, :, CW:], w_dd[:, cols])

    def source_of(way, t):
        return (x + nx - t) % nx if way == 0 else (x + t) % nx

    def from_sibling(way, t):
        source = source_of(way, t)

        @pl.when(source < nd)
        def _():
            for h in range(2):
                via = way if t < far else (0 if reach[h][0] == far else 1)
                arrived(block(source, 1 - c, h), sib_recv.at[via, t, h])
            accumulate(source, 1 - c)

    @pl.when(routes)
    def _():
        accumulate(x, c)

    for t in range(1, far + 1):
        for h in range(2):
            for way in range(2):
                if t > reach[h][way]:
                    continue
                source = source_of(way, t)

                @pl.when(source < nd)
                def _():
                    arrived(block(source, c, h), ring_recv.at[way, t, h])
                    if t < reach[h][way]:
                        remote(
                            block(source, c, h), block(source, c, h),
                            ring_send.at[way, t, h], ring_recv.at[way, t + 1, h],
                            neighbour[way],
                        ).start()
                    remote(
                        block(source, c, h), block(source, c, h), sib_send.at[way, t, h],
                        sib_recv.at[way, t, h], sibling,
                    ).start()

        for way in range(2 if t < far else 1):
            source = source_of(way, t)

            @pl.when(source < nd)
            def _():
                accumulate(source, c)

        for way in range(2 if t > 1 else 1):
            from_sibling(way, t - 1)
    from_sibling(0, far)

    both = acc_gu[...]
    turned = pltpu.roll(both, hs, 1)
    left = lax.broadcasted_iota(jnp.int32, (ns, 2 * hs), 1) < hs
    gate = jnp.where(left, both, turned)
    up = jnp.where(left, turned, both)
    sg = jax.nn.sigmoid(gate)
    active = gate * sg
    d_hidden = acc_dh[...]
    d_both = jnp.where(
        left, d_hidden * up * sg * (1.0 + gate * (1.0 - sg)), d_hidden * active
    )
    d_pair[c] = d_both.astype(BF16)
    exchange = remote(d_pair.at[c], d_pair.at[c], small_send.at[X], small_recv.at[X], sibling)
    exchange.start()
    d_t[...] = d_both.T.astype(BF16)
    h_t[...] = (active * up).T[0:hs, :].astype(BF16)

    def gradients(chunk):
        cols = slice(chunk * CW, (chunk + 1) * CW)
        grads[0 : 2 * hs, cols] = dot_nn(d_t[...], rows[chunk, :, 0:CW]).astype(BF16)
        grads[2 * hs :, cols] = dot_nn(h_t[...], rows[chunk, :, CW:]).astype(BF16)

    def partial(dest, h):
        lines = slice(h * half, (h + 1) * half)
        cols = pl.ds(pl.multiple_of((2 * dest + c) * CW, CW), CW)
        return dot_nn(d_pair[c, lines, :], w_gu[:, cols]) + dot_nn(
            d_pair[1 - c, lines, :], w_sib[dest]
        )

    def dest_of(way, d):
        return (x + d) % nx if way == 0 else (x + nx - d) % nx

    arrived(w_sib, small_recv.at[W])
    arrived(d_pair.at[0], small_recv.at[X])

    todo = list(range(nc))
    share = -(-nc // far)
    for t in range(1, far + 1):
        moves = [
            (h, way, reach[h][way] + 1 - t)
            for h in range(2)
            for way in range(2)
            if reach[h][way] + 1 - t >= 1
        ]
        if t > 1:
            for h, way, d in moves:
                dest = dest_of(way, d)

                @pl.when(dest < nd)
                def _():
                    p_buf[h, way] = partial(dest, h)

            for chunk in todo[:share]:
                gradients(chunk)
            todo = todo[share:]
        for h, way, d in moves:
            dest = dest_of(way, d)

            @pl.when(dest < nd)
            def _():
                if d == reach[h][way]:
                    value = partial(dest, h)
                else:
                    arrived(rcv.at[way, d, h], red_recv.at[way, d, h])
                    value = p_buf[h, way] + rcv[way, d, h].astype(F32)
                snd[way, d, h] = value.astype(BF16)
                remote(
                    snd.at[way, d, h], rcv.at[way, d - 1, h], red_send.at[way, d, h],
                    red_recv.at[way, d - 1, h], neighbour[way],
                ).start()

    @pl.when(routes)
    def _():
        for h in range(2):
            p_buf[h, 0] = partial(x, h)

    for chunk in todo:
        gradients(chunk)
    stores = [
        pltpu.make_async_copy(grads.at[pl.ds(0, hs)], gg.at[0], out_sem.at[0]),
        pltpu.make_async_copy(grads.at[pl.ds(hs, hs)], gu.at[0], out_sem.at[1]),
        pltpu.make_async_copy(grads.at[pl.ds(2 * hs, hs)], gd.at[0], out_sem.at[2]),
    ]
    for store in stores:
        store.start()

    @pl.when(routes)
    def _():
        for h in range(2):
            value = p_buf[h, 0]
            for way in range(2):
                if reach[h][way] >= 1:
                    arrived(rcv.at[way, 0, h], red_recv.at[way, 0, h])
                    value = value + rcv[way, 0, h].astype(F32)
            span = ng // 2
            r2_send[pl.ds(h * span, span)] = value.astype(BF16).reshape(span, cap, CW)
            for o in range(span):
                s = h * span + (z + o) % span

                @pl.when(s != z)
                def _():
                    remote(
                        r2_send.at[s], r2_recv.at[z], small_send.at[R2], small_recv.at[R2],
                        (s, m),
                    ).start()

        r2_recv[z] = r2_send[z]
        arrived(r2_recv.at[pl.ds(0, ng - 1)], small_recv.at[R2])
        summed = dot_nn(sel_t[...], r2_recv[...].reshape(ns, CW))
        r3_send[...] = summed.astype(BF16).reshape(ny, nk, CW)
        for o in range(1, ny):
            to = (y + o) % ny
            remote(
                r3_send.at[to], r3_recv.at[y], small_send.at[R3], small_recv.at[R3],
                (z, to * nk + k),
            ).start()
        r3_recv[y] = r3_send[y]
        arrived(r3_recv.at[pl.ds(0, ny - 1)], small_recv.at[R3])
        total = jnp.sum(r3_recv[...].astype(F32), axis=0)
        r4_send[:, 0, :] = total[:, 0:128]
        r4_send[:, 1, :] = total[:, 128:]
        for o in range(1, nk):
            to = (k + o) % nk
            remote(
                r4_send.at[to], r4_recv.at[k], small_send.at[R4], small_recv.at[R4],
                (z, y * nk + to),
            ).start()
        r4_recv[k] = r4_send[k]

    exchange.wait_send()
    for way in range(2):
        for h in range(2):
            for t in range(1, reach[h][way]):

                @pl.when(source_of(way, t) < nd)
                def _():
                    arrived(block(0, 0, h), ring_send.at[way, t, h])

            for t in range(1, reach[h][way] + 1):

                @pl.when(source_of(way, t) < nd)
                def _():
                    arrived(block(0, 0, h), sib_send.at[way, t, h])

                @pl.when(dest_of(way, t) < nd)
                def _():
                    arrived(snd.at[way, t, h], red_send.at[way, t, h])

    arrived(w_sib, small_send.at[W])

    @pl.when(routes)
    def _():
        for h in range(2):
            for way in range(2):
                if reach[h][way] >= 1:
                    arrived(block(0, 0, h), ring_send.at[way, 0, h])
            arrived(block(0, 0, h), sib_send.at[0, 0, h])
        arrived(recv_a.at[pl.ds(0, nc - 1)], small_send.at[A])
        arrived(t_all.at[pl.ds(0, ny - 1)], small_send.at[B])
        arrived(z_send.at[pl.ds(0, ng - 1)], small_send.at[C])
        arrived(r2_send.at[pl.ds(0, ng - 1)], small_send.at[R2])
        arrived(r3_send.at[pl.ds(0, ny - 1)], small_send.at[R3])
        arrived(r4_send.at[pl.ds(0, nk - 1)], small_send.at[R4])
        arrived(r4_recv.at[pl.ds(0, nc - 1)], small_recv.at[R4])

    @pl.when(jnp.logical_not(routes))
    def _():
        arrived(recv_a.at[pl.ds(0, nc)], small_send.at[A])
        arrived(r4_recv.at[pl.ds(0, nc)], small_recv.at[R4])

    gt_ref[...] = r4_recv[...]
    for store in stores:
        store.wait()


def shards(mesh, tokens, grad_out, route_token, route_count, route_prob, w_gate, w_up, w_down):
    ng = mesh.shape["group"]
    ny = route_token.shape[2]
    cap = route_token.shape[3]
    nk = mesh.shape["member"] // ny
    nx = nk // 2
    hs, features = w_gate.shape[1:]
    nc = features // CW
    assert nc == nk - 2 and nc * CW == features
    ns, tg, nd, half, far = ng * cap, ny * nk, nc // 2, ng * cap // 2, nx // 2
    vmem = pl.BlockSpec(memory_space=pltpu.VMEM)
    hbm = pl.BlockSpec(memory_space=pl.ANY)
    dma = pltpu.SemaphoreType.DMA
    grad_shape = jax.ShapeDtypeStruct((1, hs, features), BF16)
    grad_rows, grad_gate, grad_up, grad_down = pl.pallas_call(
        functools.partial(kernel, (ng, ny, nx, hs, cap)),
        out_shape=(
            jax.ShapeDtypeStruct((nc, 2, 128), F32),
            grad_shape,
            grad_shape,
            grad_shape,
        ),
        in_specs=[vmem] * 5 + [hbm] * 3,
        out_specs=(vmem, hbm, hbm, hbm),
        scratch_shapes=[
            pltpu.VMEM((nc, 4, 128), F32),
            pltpu.VMEM((nk, 4, 128), F32),
            pltpu.VMEM((ny, nk, 2 * CW), BF16),
            pltpu.VMEM((ng, cap, 2 * CW), BF16),
            pltpu.VMEM((nc, ns, 2 * CW), BF16),
            pltpu.VMEM((2 * hs, features), BF16),
            pltpu.VMEM((2 * hs, features), BF16),
            pltpu.VMEM((nd, 2 * hs, CW), BF16),
            pltpu.VMEM((ns, 2 * hs), F32),
            pltpu.VMEM((ns, 2 * hs), F32),
            pltpu.VMEM((tg, ns), BF16),
            pltpu.VMEM((2, ns, 2 * hs), BF16),
            pltpu.VMEM((2 * hs, ns), BF16),
            pltpu.VMEM((hs, ns), BF16),
            pltpu.VMEM((2, 2, half, CW), F32),
            pltpu.VMEM((2, far + 1, 2, half, CW), BF16),
            pltpu.VMEM((2, far, 2, half, CW), BF16),
            pltpu.VMEM((ng, cap, CW), BF16),
            pltpu.VMEM((ng, cap, CW), BF16),
            pltpu.VMEM((ny, nk, CW), BF16),
            pltpu.VMEM((ny, nk, CW), BF16),
            pltpu.VMEM((nk, 2, 128), F32),
            pltpu.VMEM((nc, 2, 128), F32),
            pltpu.VMEM((3 * hs, features), BF16),
            dma((4,)),
            dma((3,)),
            dma((8,)),
            dma((8,)),
            dma((2, far + 1, 2)),
            dma((2, far + 1, 2)),
            dma((2, far + 1, 2)),
            dma((2, far + 1, 2)),
            dma((2, far + 1, 2)),
            dma((2, far + 1, 2)),
        ],
        compiler_params=pltpu.CompilerParams(
            collective_id=0, has_side_effects=True, vmem_limit_bytes=32 * 1024 * 1024
        ),
        name="routed_backward",
    )(tokens, grad_out, route_token, route_count, route_prob, w_gate, w_up, w_down)
    return grad_rows.reshape(1, features).astype(BF16), grad_gate, grad_up, grad_down


def solution(mesh):
    both = ("group", "member")
    return jax.shard_map(
        functools.partial(shards, mesh),
        mesh=mesh,
        in_specs=(
            P(both, None),
            P(both, None),
            P("group", None, None, None),
            P("group", None, None),
            P("group", None, None, None),
            P(both, None, None),
            P(both, None, None),
            P(both, None, None),
        ),
        out_specs=(
            P(both, None),
            P(both, None, None),
            P(both, None, None),
            P(both, None, None),
        ),
        check_vma=False,
    )
```

```python
import functools

import jax
import jax.numpy as jnp
from jax import lax
from jax.experimental import pallas as pl
from jax.experimental.pallas import tpu as pltpu
from jax.sharding import PartitionSpec as P

MESH = pl.DeviceIdType.MESH
CLASSES = 4
LANES = 128
F32 = jnp.float32
BF16 = jnp.bfloat16


def dot_nn(a, b):
    return jnp.dot(a, b, preferred_element_type=F32)


def dot_nt(a, b):
    return lax.dot_general(a, b, (((1,), (1,)), ((), ())), preferred_element_type=F32)


def kernel(
    dims,
    x_hbm, dy_hbm, tok_hbm, cnt_hbm, prob_hbm, wg, wu, wd,
    gt_ref, gg, gu, gd,
    x_ref, dy_ref, tok_ref, cnt_ref, prob_ref,
    send_a, recv_a, t_all, z_send, rows, w_gu, w_dd, w_sib, acc_gu, acc_dh,
    d_pair, d_t, h_t, p_buf, snd, rcv, r2_send, r2_recv, r3_send, r3_recv,
    r4_send, r4_recv,
    in_sem, w_sem, small_send, small_recv, ring_send, ring_recv, sib_send, sib_recv,
    red_send, red_recv,
):
    ng, ny, nx, hs, cap, cw = dims
    nk = 2 * nx
    ns = ng * cap
    tg = ny * nk
    half = ns // 2
    span = ng // 2
    units = cw // LANES
    pieces = [slice(o, min(o + 256, cw)) for o in range(0, cw, 256)]

    z = lax.axis_index("group")
    m = lax.axis_index("member")
    y = m // nk
    k = m % nk
    x = k // 2
    c = k % 2
    brings = x % CLASSES
    own = k % CLASSES
    other = (own + 2) % CLASSES
    sibling = (z, y * nk + 2 * x + (1 - c))

    def along(steps):
        return (z, y * nk + 2 * ((x + steps + nx) % nx) + c)

    neighbour = (along(1), along(-1))

    def remote(src, dst, send_sem, recv_sem, device):
        return pltpu.make_async_remote_copy(
            src_ref=src, dst_ref=dst, send_sem=send_sem, recv_sem=recv_sem,
            device_id=device, device_id_type=MESH,
        )

    def arrived(ref, sem):
        pltpu.make_async_copy(ref, ref, sem).wait()

    def signal(device):
        pl.semaphore_signal(
            pltpu.get_barrier_semaphore(), inc=1, device_id=device, device_id_type=MESH
        )

    A, B, C, W, X, R2, R3, R4 = range(8)

    for o in range(1, nk):
        signal((z, y * nk + (k + o) % nk))
    for o in range(1, ny):
        signal((z, ((y + o) % ny) * nk + k))
    for o in range(1, ng):
        signal(((z + o) % ng, m))

    inputs = [
        pltpu.make_async_copy(src, dst, in_sem.at[i])
        for i, (src, dst) in enumerate(
            (
                (x_hbm, x_ref), (dy_hbm, dy_ref), (tok_hbm, tok_ref), (cnt_hbm, cnt_ref),
                (prob_hbm, prob_ref),
            )
        )
    ]
    for copy in inputs:
        copy.start()
    loads = [
        pltpu.make_async_copy(wg.at[0], w_gu.at[pl.ds(0, hs)], w_sem.at[0]),
        pltpu.make_async_copy(wu.at[0], w_gu.at[pl.ds(hs, hs)], w_sem.at[1]),
        pltpu.make_async_copy(wd.at[0], w_dd.at[pl.ds(0, hs)], w_sem.at[2]),
        pltpu.make_async_copy(wd.at[0], w_dd.at[pl.ds(hs, hs)], w_sem.at[3]),
    ]
    for load in loads:
        load.start()
    for copy in inputs:
        copy.wait()

    send_a[...] = jnp.zeros_like(send_a)
    for u in range(CLASSES * units):
        cols = slice(u * LANES, (u + 1) * LANES)
        send_a[u // units, pl.ds(u % units, 1), :] = x_ref[:, cols].astype(F32)
        send_a[CLASSES + u // units, pl.ds(u % units, 1), :] = dy_ref[:, cols].astype(F32)

    pl.semaphore_wait(pltpu.get_barrier_semaphore(), (nk - 1) + (ny - 1) + (ng - 1))

    for o in range(1, nk):
        kk = (k + o) % nk
        remote(
            send_a.at[(kk % 2) * CLASSES + kk // 2 % CLASSES], recv_a.at[k], small_send.at[A], small_recv.at[A],
            (z, y * nk + kk),
        ).start()
    recv_a[k] = send_a[c * CLASSES + brings]

    row = lax.broadcasted_iota(jnp.int32, (ns, cap), 0)
    lane = lax.broadcasted_iota(jnp.int32, (ns, cap), 1)

    def spread(ref):
        wide = jnp.concatenate(
            [
                jnp.broadcast_to(ref[0, i, pl.ds(y, 1), :].astype(F32), (cap, cap))
                for i in range(ng)
            ],
            axis=0,
        )
        return jnp.sum(jnp.where(lane == row % cap, wide, 0.0), axis=1, keepdims=True)

    counts = jnp.concatenate(
        [
            jnp.broadcast_to(cnt_ref[0, pl.ds(i, 1), :].astype(F32), (cap, ny))
            for i in range(ng)
        ],
        axis=0,
    )
    expert = lax.broadcasted_iota(jnp.int32, (ns, ny), 1)
    counts = jnp.sum(jnp.where(expert == y, counts, 0.0), axis=1, keepdims=True)
    slot_token = spread(tok_ref)
    position = (lax.broadcasted_iota(jnp.int32, (ns, 1), 0) % cap).astype(F32)
    live = jnp.where(position < counts, 1.0, 0.0)
    core = c.astype(F32)
    factor = spread(prob_ref) * live * core + (1.0 - core)
    token = lax.broadcasted_iota(jnp.int32, (ns, tg), 1).astype(F32)
    sel = jnp.where(token == slot_token, 1.0, 0.0)
    sel_t = (sel * live).T.astype(BF16)
    sel = sel.astype(BF16)

    for load in loads:
        load.wait()
    for i in range(2):
        cols = pl.ds(pl.multiple_of((2 * i + 1 - c) * cw, LANES), cw)
        remote(
            w_gu.at[:, cols], w_sib.at[i], small_send.at[W], small_recv.at[W], sibling
        ).start()

    acc_gu[...] = jnp.zeros_like(acc_gu)
    acc_dh[...] = jnp.zeros_like(acc_dh)

    arrived(recv_a.at[pl.ds(0, nk - 1)], small_recv.at[A])
    t_all[y] = jnp.concatenate([recv_a[:, u, :] for u in range(units)], axis=1).astype(BF16)
    for o in range(1, ny):
        remote(
            t_all.at[y], t_all.at[y], small_send.at[B], small_recv.at[B],
            (z, ((y + o) % ny) * nk + k),
        ).start()
    arrived(t_all.at[pl.ds(0, ny - 1)], small_recv.at[B])
    for piece in pieces:
        width = piece.stop - piece.start
        picked = dot_nn(sel, t_all[:, :, piece].reshape(tg, width)) * factor
        z_send[:, :, piece] = picked.astype(BF16).reshape(ng, cap, width)
    here = pl.ds(pl.multiple_of(z * cap, cap), cap)
    for o in range(1, ng):
        g = (z + o) % ng
        remote(
            z_send.at[g], rows.at[c, brings, here, :], small_send.at[C], small_recv.at[C],
            (g, m),
        ).start()
    rows[c, brings, here, :] = z_send[z]
    arrived(rows.at[c, brings, pl.ds(0, ns - cap), :], small_recv.at[C])

    whole, first, second = pl.ds(0, ns), pl.ds(0, half), pl.ds(half, half)
    moves = ((1, whole), (-1, whole), (2, first), (-2, second))
    for i, (steps, part) in enumerate(moves):
        block = rows.at[c, brings, part, :]
        remote(block, block, ring_send.at[i], ring_recv.at[i], along(steps)).start()

    def share(quarter, part, i):
        block = rows.at[c, quarter, part, :]
        return remote(block, block, sib_send.at[i], sib_recv.at[i], sibling)

    def accumulate(quarter):
        cols = pl.ds(pl.multiple_of(quarter * cw, LANES), cw)
        acc_gu[...] += dot_nt(rows[0, quarter], w_gu[:, cols])
        acc_dh[...] += dot_nt(rows[1, quarter], w_dd[:, cols])

    def source(steps):
        return (brings + CLASSES - steps) % CLASSES

    share(brings, whole, 4).start()
    arrived(rows.at[1 - c, brings], sib_recv.at[4])
    accumulate(brings)
    for stage in (0, 2):
        for i in (stage, stage + 1):
            steps, part = moves[i]
            arrived(rows.at[c, source(steps), part, :], ring_recv.at[i])
            share(source(steps), part, i).start()
        for i in (stage, stage + 1):
            steps, part = moves[i]
            arrived(rows.at[1 - c, source(steps), part, :], sib_recv.at[i])
            if i != 2:
                accumulate(source(steps))

    both = acc_gu[...]
    turned = pltpu.roll(both, hs, 1)
    left = lax.broadcasted_iota(jnp.int32, (ns, 2 * hs), 1) < hs
    gate = jnp.where(left, both, turned)
    up = jnp.where(left, turned, both)
    sg = jax.nn.sigmoid(gate)
    active = gate * sg
    d_hidden = acc_dh[...]
    d_both = jnp.where(
        left, d_hidden * up * sg * (1.0 + gate * (1.0 - sg)), d_hidden * active
    )
    d_pair[c] = d_both.astype(BF16)
    exchange = remote(d_pair.at[c], d_pair.at[c], small_send.at[X], small_recv.at[X], sibling)
    exchange.start()
    d_t[...] = d_both.T.astype(BF16)
    h_t[...] = (active * up).T[0:hs, :].astype(BF16)

    def gradients(quarter):
        for piece in pieces:
            cols = slice(quarter * cw + piece.start, quarter * cw + piece.stop)
            pair = dot_nn(d_t[...], rows[0, quarter, :, piece]).astype(BF16)
            gg[0, :, cols] = pair[0:hs]
            gu[0, :, cols] = pair[hs:]
            gd[0, :, cols] = dot_nn(h_t[...], rows[1, quarter, :, piece]).astype(BF16)

    def partial(quarter, h, piece):
        lines = slice(h * half, (h + 1) * half)
        width = piece.stop - piece.start
        cols = pl.ds(pl.multiple_of(quarter * cw + piece.start, LANES), width)
        return dot_nn(d_pair[c, lines, :], w_gu[:, cols]) + dot_nn(
            d_pair[1 - c, lines, :], w_sib[quarter // 2, :, piece]
        )

    arrived(w_sib, small_recv.at[W])
    arrived(d_pair.at[0], small_recv.at[X])

    for h in range(2):
        for piece in pieces:
            snd[h, :, piece] = partial(other, h, piece).astype(BF16)
        remote(snd.at[h], rcv.at[h], red_send.at[h], red_recv.at[h], neighbour[h]).start()
    for h in range(2):
        for piece in pieces:
            p_buf[h, :, piece] = partial(own, h, piece)
    gradients(0)
    gradients(1)

    for h in range(2):
        arrived(rcv.at[h], red_recv.at[h])
        value = p_buf[h] + rcv[h].astype(F32)
        r2_send[pl.ds(h * span, span)] = value.astype(BF16).reshape(span, cap, cw)
        for o in range(span):
            s = h * span + (z + o) % span

            @pl.when(s != z)
            def _():
                remote(
                    r2_send.at[s], r2_recv.at[z], small_send.at[R2], small_recv.at[R2], (s, m)
                ).start()

    r2_recv[z] = r2_send[z]
    gradients(2)
    gradients(3)
    arrived(r2_recv.at[pl.ds(0, ng - 1)], small_recv.at[R2])
    for piece in pieces:
        width = piece.stop - piece.start
        summed = dot_nn(sel_t, r2_recv[:, :, piece].reshape(ns, width))
        r3_send[:, :, piece] = summed.astype(BF16).reshape(ny, nk, width)
    for o in range(1, ny):
        to = (y + o) % ny
        remote(
            r3_send.at[to], r3_recv.at[y], small_send.at[R3], small_recv.at[R3],
            (z, to * nk + k),
        ).start()
    r3_recv[y] = r3_send[y]
    r4_send[...] = jnp.zeros_like(r4_send)

    arrived(recv_a.at[pl.ds(0, nk - 1)], small_send.at[A])
    arrived(t_all.at[pl.ds(0, ny - 1)], small_send.at[B])
    arrived(z_send.at[pl.ds(0, ng - 1)], small_send.at[C])
    arrived(w_sib, small_send.at[W])
    for i, (steps, part) in enumerate(moves):
        arrived(rows.at[0, 0, part, :], ring_send.at[i])
        arrived(rows.at[0, 0, part, :], sib_send.at[i])
    arrived(rows.at[0, 0], sib_send.at[4])
    for h in range(2):
        arrived(snd.at[h], red_send.at[h])
    exchange.wait_send()
    arrived(r2_send.at[pl.ds(0, ng - 1)], small_send.at[R2])

    arrived(r3_recv.at[pl.ds(0, ny - 1)], small_recv.at[R3])
    for u in range(units):
        cols = slice(u * LANES, (u + 1) * LANES)
        r4_send[:, u, :] = jnp.sum(r3_recv[:, :, cols].astype(F32), axis=0)
    for o in range(1, nk):
        to = (k + o) % nk
        remote(
            r4_send.at[to], r4_recv.at[k], small_send.at[R4], small_recv.at[R4],
            (z, y * nk + to),
        ).start()
    r4_recv[k] = r4_send[k]
    arrived(r3_send.at[pl.ds(0, ny - 1)], small_send.at[R3])
    arrived(r4_recv.at[pl.ds(0, nk - 1)], small_recv.at[R4])
    for quarter in range(CLASSES):
        total = r4_recv[quarter]
        for k2 in range(quarter + CLASSES, nk, CLASSES):
            total = total + r4_recv[k2]
        for u in range(units):
            cols = slice((quarter * units + u) * LANES, (quarter * units + u + 1) * LANES)
            gt_ref[:, cols] = total[u : u + 1, :].astype(BF16)
    arrived(r4_send.at[pl.ds(0, nk - 1)], small_send.at[R4])


def shards(mesh, tokens, grad_out, route_token, route_count, route_prob, w_gate, w_up, w_down):
    ng = mesh.shape["group"]
    ny = route_token.shape[2]
    cap = route_token.shape[3]
    nk = mesh.shape["member"] // ny
    hs, features = w_gate.shape[1:]
    cw = features // CLASSES
    assert cw % LANES == 0 and nk % (2 * CLASSES) == 0
    ns, tg, half, units = ng * cap, ny * nk, ng * cap // 2, cw // LANES
    low = -(-units // 8) * 8
    vmem = pl.BlockSpec(memory_space=pltpu.VMEM)
    hbm = pl.BlockSpec(memory_space=pl.ANY)
    dma = pltpu.SemaphoreType.DMA
    grad_shape = jax.ShapeDtypeStruct((1, hs, features), BF16)
    operands = (tokens, grad_out, route_token, route_count, route_prob, w_gate, w_up, w_down)
    return pl.pallas_call(
        functools.partial(kernel, (ng, ny, nk // 2, hs, cap, cw)),
        out_shape=(
            jax.ShapeDtypeStruct((1, features), BF16),
            grad_shape,
            grad_shape,
            grad_shape,
        ),
        in_specs=[hbm] * 8,
        out_specs=(vmem,) * 4,
        scratch_shapes=[
            pltpu.VMEM((1, features), BF16),
            pltpu.VMEM((1, features), BF16),
            pltpu.VMEM(route_token.shape, jnp.int32),
            pltpu.VMEM(route_count.shape, jnp.int32),
            pltpu.VMEM(route_prob.shape, F32),
            pltpu.VMEM((2 * CLASSES, low, LANES), F32),
            pltpu.VMEM((nk, low, LANES), F32),
            pltpu.VMEM((ny, nk, cw), BF16),
            pltpu.VMEM((ng, cap, cw), BF16),
            pltpu.VMEM((2, CLASSES, ns, cw), BF16),
            pltpu.VMEM((2 * hs, features), BF16),
            pltpu.VMEM((2 * hs, features), BF16),
            pltpu.VMEM((2, 2 * hs, cw), BF16),
            pltpu.VMEM((ns, 2 * hs), F32),
            pltpu.VMEM((ns, 2 * hs), F32),
            pltpu.VMEM((2, ns, 2 * hs), BF16),
            pltpu.VMEM((2 * hs, ns), BF16),
            pltpu.VMEM((hs, ns), BF16),
            pltpu.VMEM((2, half, cw), F32),
            pltpu.VMEM((2, half, cw), BF16),
            pltpu.VMEM((2, half, cw), BF16),
            pltpu.VMEM((ng, cap, cw), BF16),
            pltpu.VMEM((ng, cap, cw), BF16),
            pltpu.VMEM((ny, nk, cw), BF16),
            pltpu.VMEM((ny, nk, cw), BF16),
            pltpu.VMEM((nk, low, LANES), F32),
            pltpu.VMEM((nk, low, LANES), F32),
            dma((5,)),
            dma((4,)),
            dma((8,)),
            dma((8,)),
            dma((4,)),
            dma((4,)),
            dma((5,)),
            dma((5,)),
            dma((2,)),
            dma((2,)),
        ],
        compiler_params=pltpu.CompilerParams(
            collective_id=0, has_side_effects=True, vmem_limit_bytes=32 * 1024 * 1024
        ),
        name="routed_backward",
    )(*[pltpu.with_memory_space_constraint(a, pltpu.HBM) for a in operands])


def solution(mesh):
    both = ("group", "member")
    return jax.shard_map(
        functools.partial(shards, mesh),
        mesh=mesh,
        in_specs=(
            P(both, None),
            P(both, None),
            P("group", None, None, None),
            P("group", None, None),
            P("group", None, None, None),
            P(both, None, None),
            P(both, None, None),
            P(both, None, None),
        ),
        out_specs=(
            P(both, None),
            P(both, None, None),
            P(both, None, None),
            P(both, None, None),
        ),
        check_vma=False,
    )
```

```python
import functools

import jax
import jax.numpy as jnp
from jax import lax
from jax.experimental import pallas as pl
from jax.experimental.pallas import tpu as pltpu
from jax.sharding import PartitionSpec as P

MESH = pl.DeviceIdType.MESH
CLASSES = 4
LANES = 128
F32 = jnp.float32
BF16 = jnp.bfloat16


def dot_nn(a, b):
    return jnp.dot(a, b, preferred_element_type=F32)


def dot_nt(a, b):
    return lax.dot_general(a, b, (((1,), (1,)), ((), ())), preferred_element_type=F32)


def far_first(n):
    return sorted(range(1, n), key=lambda o: -min(o, n - o))


def kernel(
    dims,
    x_hbm, dy_hbm, tok_hbm, cnt_hbm, prob_hbm, wg, wu, wd,
    gt_ref, gg, gu, gd,
    x_ref, dy_ref, tok_ref, cnt_ref, prob_ref,
    send_a, recv_a, t_all, z_send, rows, w_gu, w_dd, w_sib, acc_gu, acc_dh,
    d_pair, d_t, h_t, p_buf, snd, rcv, r2_send, r2_recv, r3_send, r3_recv,
    r4_send, r4_recv,
    in_sem, w_sem, small_send, small_recv, ring_send, ring_recv, sib_send, sib_recv,
    red_send, red_recv,
):
    ng, ny, nx, hs, cap, cw = dims
    nk = 2 * nx
    ns = ng * cap
    tg = ny * nk
    half = ns // 2
    span = ng // 2
    units = cw // LANES
    cut = -(-units // 2) * LANES
    parts = (pl.ds(0, cut), pl.ds(cut, cw - cut))
    pieces = [
        [slice(o, min(o + 256, hi)) for o in range(lo, hi, 256)]
        for lo, hi in ((0, cut), (cut, cw))
    ]

    z = lax.axis_index("group")
    m = lax.axis_index("member")
    y = m // nk
    k = m % nk
    x = k // 2
    c = k % 2
    brings = x % CLASSES
    own = k % CLASSES
    other = (own + 2) % CLASSES
    sibling = (z, y * nk + 2 * x + (1 - c))

    def along(steps):
        return (z, y * nk + 2 * ((x + steps + nx) % nx) + c)

    neighbour = (along(1), along(-1))

    def remote(src, dst, send_sem, recv_sem, device):
        return pltpu.make_async_remote_copy(
            src_ref=src, dst_ref=dst, send_sem=send_sem, recv_sem=recv_sem,
            device_id=device, device_id_type=MESH,
        )

    def arrived(ref, sem):
        pltpu.make_async_copy(ref, ref, sem).wait()

    def signal(device):
        pl.semaphore_signal(
            pltpu.get_barrier_semaphore(), inc=1, device_id=device, device_id_type=MESH
        )

    A, W, X, R4, B, C, R2, R3 = 0, 1, 2, 3, 4, 6, 8, 10

    for o in far_first(nk):
        signal((z, y * nk + (k + o) % nk))
    for o in far_first(ny):
        signal((z, ((y + o) % ny) * nk + k))
    for o in far_first(ng):
        signal(((z + o) % ng, m))

    inputs = [
        pltpu.make_async_copy(src, dst, in_sem.at[i])
        for i, (src, dst) in enumerate(
            (
                (x_hbm, x_ref), (dy_hbm, dy_ref), (tok_hbm, tok_ref), (cnt_hbm, cnt_ref),
                (prob_hbm, prob_ref),
            )
        )
    ]
    for copy in inputs:
        copy.start()
    loads = [
        pltpu.make_async_copy(wg.at[0], w_gu.at[pl.ds(0, hs)], w_sem.at[0]),
        pltpu.make_async_copy(wu.at[0], w_gu.at[pl.ds(hs, hs)], w_sem.at[1]),
        pltpu.make_async_copy(wd.at[0], w_dd.at[pl.ds(0, hs)], w_sem.at[2]),
        pltpu.make_async_copy(wd.at[0], w_dd.at[pl.ds(hs, hs)], w_sem.at[3]),
    ]
    for load in loads:
        load.start()
    for copy in inputs:
        copy.wait()

    send_a[...] = jnp.zeros_like(send_a)
    for u in range(CLASSES * units):
        cols = slice(u * LANES, (u + 1) * LANES)
        send_a[u // units, pl.ds(u % units, 1), :] = x_ref[:, cols].astype(F32)
        send_a[CLASSES + u // units, pl.ds(u % units, 1), :] = dy_ref[:, cols].astype(F32)

    pl.semaphore_wait(pltpu.get_barrier_semaphore(), (nk - 1) + (ny - 1) + (ng - 1))

    for o in far_first(nk):
        kk = (k + o) % nk
        remote(
            send_a.at[(kk % 2) * CLASSES + kk // 2 % CLASSES], recv_a.at[k], small_send.at[A], small_recv.at[A],
            (z, y * nk + kk),
        ).start()
    recv_a[k] = send_a[c * CLASSES + brings]

    row = lax.broadcasted_iota(jnp.int32, (ns, cap), 0)
    lane = lax.broadcasted_iota(jnp.int32, (ns, cap), 1)

    def spread(ref):
        wide = jnp.concatenate(
            [
                jnp.broadcast_to(ref[0, i, pl.ds(y, 1), :].astype(F32), (cap, cap))
                for i in range(ng)
            ],
            axis=0,
        )
        return jnp.sum(jnp.where(lane == row % cap, wide, 0.0), axis=1, keepdims=True)

    counts = jnp.concatenate(
        [
            jnp.broadcast_to(cnt_ref[0, pl.ds(i, 1), :].astype(F32), (cap, ny))
            for i in range(ng)
        ],
        axis=0,
    )
    expert = lax.broadcasted_iota(jnp.int32, (ns, ny), 1)
    counts = jnp.sum(jnp.where(expert == y, counts, 0.0), axis=1, keepdims=True)
    slot_token = spread(tok_ref)
    position = (lax.broadcasted_iota(jnp.int32, (ns, 1), 0) % cap).astype(F32)
    live = jnp.where(position < counts, 1.0, 0.0)
    core = c.astype(F32)
    factor = spread(prob_ref) * live * core + (1.0 - core)
    token = lax.broadcasted_iota(jnp.int32, (ns, tg), 1).astype(F32)
    sel = jnp.where(token == slot_token, 1.0, 0.0)
    sel_t = (sel * live).T.astype(BF16)
    sel = sel.astype(BF16)

    for load in loads:
        load.wait()
    for i in range(2):
        cols = pl.ds(pl.multiple_of((2 * i + 1 - c) * cw, LANES), cw)
        remote(
            w_gu.at[:, cols], w_sib.at[i], small_send.at[W], small_recv.at[W], sibling
        ).start()

    acc_gu[...] = jnp.zeros_like(acc_gu)
    acc_dh[...] = jnp.zeros_like(acc_dh)

    arrived(recv_a.at[pl.ds(0, nk - 1)], small_recv.at[A])
    t_all[y] = jnp.concatenate([recv_a[:, u, :] for u in range(units)], axis=1).astype(BF16)
    for p, part in enumerate(parts):
        if p:
            arrived(t_all.at[pl.ds(0, ny - 1), :, parts[0]], small_send.at[B])
        for o in far_first(ny):
            block = t_all.at[y, :, part]
            remote(
                block, block, small_send.at[B + p], small_recv.at[B + p],
                (z, ((y + o) % ny) * nk + k),
            ).start()
    here = pl.ds(pl.multiple_of(z * cap, cap), cap)
    for p, part in enumerate(parts):
        arrived(t_all.at[pl.ds(0, ny - 1), :, part], small_recv.at[B + p])
        for piece in pieces[p]:
            width = piece.stop - piece.start
            picked = dot_nn(sel, t_all[:, :, piece].reshape(tg, width)) * factor
            z_send[:, :, piece] = picked.astype(BF16).reshape(ng, cap, width)
        if p:
            arrived(z_send.at[pl.ds(0, ng - 1), :, parts[0]], small_send.at[C])
        for o in far_first(ng):
            g = (z + o) % ng
            remote(
                z_send.at[g, :, part], rows.at[c, brings, here, part],
                small_send.at[C + p], small_recv.at[C + p], (g, m),
            ).start()
    rows[c, brings, here, :] = z_send[z]

    moves = ((1, 0), (-1, 0), (1, 1), (-1, 1), (2, 0), (-2, 1))
    goes_on = {0: 4, 3: 5}

    def source(steps):
        return (brings + CLASSES - steps) % CLASSES

    def pass_on(quarter, i):
        steps, p = moves[i]
        block = rows.at[c, quarter, :, parts[p]]
        remote(
            block, block, ring_send.at[i], ring_recv.at[i], along(1 if steps > 0 else -1)
        ).start()

    def share(quarter, p, i):
        block = rows.at[c, quarter, :, parts[p]]
        remote(block, block, sib_send.at[i], sib_recv.at[i], sibling).start()

    def accumulate(quarter):
        cols = pl.ds(pl.multiple_of(quarter * cw, LANES), cw)
        acc_gu[...] += dot_nt(rows[0, quarter], w_gu[:, cols])
        acc_dh[...] += dot_nt(rows[1, quarter], w_dd[:, cols])

    for p, part in enumerate(parts):
        arrived(rows.at[c, brings, pl.ds(0, ns - cap), part], small_recv.at[C + p])
        if p:
            for i in (0, 1):
                arrived(rows.at[0, 0, :, parts[0]], ring_send.at[i])
        pass_on(brings, 2 * p)
        pass_on(brings, 2 * p + 1)
        share(brings, p, 6 + p)
    for i in range(6):
        steps, p = moves[i]
        arrived(rows.at[c, source(steps), :, parts[p]], ring_recv.at[i])
        if i in goes_on:
            pass_on(source(steps), goes_on[i])
        share(source(steps), p, i)
        if i == 1:
            for p in range(2):
                arrived(rows.at[1 - c, brings, :, parts[p]], sib_recv.at[6 + p])
            accumulate(brings)
        if i in (3, 5):
            for j in (0, 1, 2, 3) if i == 3 else (4, 5):
                steps, p = moves[j]
                arrived(rows.at[1 - c, source(steps), :, parts[p]], sib_recv.at[j])
                if j in (2, 3, 5):
                    accumulate(source(steps))

    both = acc_gu[...]
    turned = pltpu.roll(both, hs, 1)
    left = lax.broadcasted_iota(jnp.int32, (ns, 2 * hs), 1) < hs
    gate = jnp.where(left, both, turned)
    up = jnp.where(left, turned, both)
    sg = jax.nn.sigmoid(gate)
    active = gate * sg
    d_hidden = acc_dh[...]
    d_both = jnp.where(
        left, d_hidden * up * sg * (1.0 + gate * (1.0 - sg)), d_hidden * active
    )
    d_pair[c] = d_both.astype(BF16)
    exchange = remote(d_pair.at[c], d_pair.at[c], small_send.at[X], small_recv.at[X], sibling)
    exchange.start()
    d_t[...] = d_both.T.astype(BF16)
    h_t[...] = (active * up).T[0:hs, :].astype(BF16)

    def gradients(quarter):
        for piece in pieces[0] + pieces[1]:
            cols = slice(quarter * cw + piece.start, quarter * cw + piece.stop)
            pair = dot_nn(d_t[...], rows[0, quarter, :, piece]).astype(BF16)
            gg[0, :, cols] = pair[0:hs]
            gu[0, :, cols] = pair[hs:]
            gd[0, :, cols] = dot_nn(h_t[...], rows[1, quarter, :, piece]).astype(BF16)

    def partial(quarter, h, piece):
        lines = slice(h * half, (h + 1) * half)
        width = piece.stop - piece.start
        cols = pl.ds(pl.multiple_of(quarter * cw + piece.start, LANES), width)
        return dot_nn(d_pair[c, lines, :], w_gu[:, cols]) + dot_nn(
            d_pair[1 - c, lines, :], w_sib[quarter // 2, :, piece]
        )

    arrived(w_sib, small_recv.at[W])
    arrived(d_pair.at[0], small_recv.at[X])

    for p, part in enumerate(parts):
        for h in range(2):
            for piece in pieces[p]:
                snd[h, :, piece] = partial(other, h, piece).astype(BF16)
            if p:
                arrived(snd.at[h, :, parts[0]], red_send.at[0, h])
            remote(
                snd.at[h, :, part], rcv.at[h, :, part], red_send.at[p, h], red_recv.at[p, h],
                neighbour[h],
            ).start()
    for h in range(2):
        for piece in pieces[0] + pieces[1]:
            p_buf[h, :, piece] = partial(own, h, piece)
    gradients(0)

    for p, part in enumerate(parts):
        for h in range(2):
            arrived(rcv.at[h, :, part], red_recv.at[p, h])
            for piece in pieces[p]:
                value = p_buf[h, :, piece] + rcv[h, :, piece].astype(F32)
                r2_send[pl.ds(h * span, span), :, piece] = value.astype(BF16).reshape(
                    span, cap, piece.stop - piece.start
                )
        if p:
            arrived(r2_send.at[pl.ds(0, ng - 1), :, parts[0]], small_send.at[R2])
        for o in far_first(ng):
            s = (z + o) % ng
            remote(
                r2_send.at[s, :, part], r2_recv.at[z, :, part], small_send.at[R2 + p],
                small_recv.at[R2 + p], (s, m),
            ).start()
    r2_recv[z] = r2_send[z]
    gradients(1)
    gradients(2)
    for p, part in enumerate(parts):
        arrived(r2_recv.at[pl.ds(0, ng - 1), :, part], small_recv.at[R2 + p])
        for piece in pieces[p]:
            width = piece.stop - piece.start
            summed = dot_nn(sel_t, r2_recv[:, :, piece].reshape(ns, width))
            r3_send[:, :, piece] = summed.astype(BF16).reshape(ny, nk, width)
        if p:
            arrived(r3_send.at[pl.ds(0, ny - 1), :, parts[0]], small_send.at[R3])
        for o in far_first(ny):
            to = (y + o) % ny
            remote(
                r3_send.at[to, :, part], r3_recv.at[y, :, part], small_send.at[R3 + p],
                small_recv.at[R3 + p], (z, to * nk + k),
            ).start()
    r3_recv[y] = r3_send[y]
    gradients(3)
    r4_send[...] = jnp.zeros_like(r4_send)

    arrived(recv_a.at[pl.ds(0, nk - 1)], small_send.at[A])
    arrived(t_all.at[pl.ds(0, ny - 1), :, parts[1]], small_send.at[B + 1])
    arrived(z_send.at[pl.ds(0, ng - 1), :, parts[1]], small_send.at[C + 1])
    arrived(w_sib, small_send.at[W])
    for i, (steps, p) in enumerate(moves):
        if i > 1:
            arrived(rows.at[0, 0, :, parts[p]], ring_send.at[i])
        arrived(rows.at[0, 0, :, parts[p]], sib_send.at[i])
    for p, part in enumerate(parts):
        arrived(rows.at[0, 0, :, part], sib_send.at[6 + p])
    for h in range(2):
        arrived(snd.at[h, :, parts[1]], red_send.at[1, h])
    exchange.wait_send()
    arrived(r2_send.at[pl.ds(0, ng - 1), :, parts[1]], small_send.at[R2 + 1])

    for p, part in enumerate(parts):
        arrived(r3_recv.at[pl.ds(0, ny - 1), :, part], small_recv.at[R3 + p])
        for u in range(p * cut // LANES, units if p else cut // LANES):
            cols = slice(u * LANES, (u + 1) * LANES)
            r4_send[:, u, :] = jnp.sum(r3_recv[:, :, cols].astype(F32), axis=0)
    for o in far_first(nk):
        to = (k + o) % nk
        remote(
            r4_send.at[to], r4_recv.at[k], small_send.at[R4], small_recv.at[R4],
            (z, y * nk + to),
        ).start()
    r4_recv[k] = r4_send[k]
    arrived(r3_send.at[pl.ds(0, ny - 1), :, parts[1]], small_send.at[R3 + 1])
    arrived(r4_recv.at[pl.ds(0, nk - 1)], small_recv.at[R4])
    for quarter in range(CLASSES):
        total = r4_recv[quarter]
        for k2 in range(quarter + CLASSES, nk, CLASSES):
            total = total + r4_recv[k2]
        for u in range(units):
            cols = slice((quarter * units + u) * LANES, (quarter * units + u + 1) * LANES)
            gt_ref[:, cols] = total[u : u + 1, :].astype(BF16)
    arrived(r4_send.at[pl.ds(0, nk - 1)], small_send.at[R4])


def shards(mesh, tokens, grad_out, route_token, route_count, route_prob, w_gate, w_up, w_down):
    ng = mesh.shape["group"]
    ny = route_token.shape[2]
    cap = route_token.shape[3]
    nk = mesh.shape["member"] // ny
    hs, features = w_gate.shape[1:]
    cw = features // CLASSES
    assert cw % LANES == 0 and nk % (2 * CLASSES) == 0
    ns, tg, half, units = ng * cap, ny * nk, ng * cap // 2, cw // LANES
    low = -(-units // 8) * 8
    vmem = pl.BlockSpec(memory_space=pltpu.VMEM)
    hbm = pl.BlockSpec(memory_space=pl.ANY)
    dma = pltpu.SemaphoreType.DMA
    grad_shape = jax.ShapeDtypeStruct((1, hs, features), BF16)
    operands = (tokens, grad_out, route_token, route_count, route_prob, w_gate, w_up, w_down)
    return pl.pallas_call(
        functools.partial(kernel, (ng, ny, nk // 2, hs, cap, cw)),
        out_shape=(
            jax.ShapeDtypeStruct((1, features), BF16),
            grad_shape,
            grad_shape,
            grad_shape,
        ),
        in_specs=[hbm] * 8,
        out_specs=(vmem,) * 4,
        scratch_shapes=[
            pltpu.VMEM((1, features), BF16),
            pltpu.VMEM((1, features), BF16),
            pltpu.VMEM(route_token.shape, jnp.int32),
            pltpu.VMEM(route_count.shape, jnp.int32),
            pltpu.VMEM(route_prob.shape, F32),
            pltpu.VMEM((2 * CLASSES, low, LANES), F32),
            pltpu.VMEM((nk, low, LANES), F32),
            pltpu.VMEM((ny, nk, cw), BF16),
            pltpu.VMEM((ng, cap, cw), BF16),
            pltpu.VMEM((2, CLASSES, ns, cw), BF16),
            pltpu.VMEM((2 * hs, features), BF16),
            pltpu.VMEM((2 * hs, features), BF16),
            pltpu.VMEM((2, 2 * hs, cw), BF16),
            pltpu.VMEM((ns, 2 * hs), F32),
            pltpu.VMEM((ns, 2 * hs), F32),
            pltpu.VMEM((2, ns, 2 * hs), BF16),
            pltpu.VMEM((2 * hs, ns), BF16),
            pltpu.VMEM((hs, ns), BF16),
            pltpu.VMEM((2, half, cw), F32),
            pltpu.VMEM((2, half, cw), BF16),
            pltpu.VMEM((2, half, cw), BF16),
            pltpu.VMEM((ng, cap, cw), BF16),
            pltpu.VMEM((ng, cap, cw), BF16),
            pltpu.VMEM((ny, nk, cw), BF16),
            pltpu.VMEM((ny, nk, cw), BF16),
            pltpu.VMEM((nk, low, LANES), F32),
            pltpu.VMEM((nk, low, LANES), F32),
            dma((5,)),
            dma((4,)),
            dma((12,)),
            dma((12,)),
            dma((6,)),
            dma((6,)),
            dma((8,)),
            dma((8,)),
            dma((2, 2)),
            dma((2, 2)),
        ],
        compiler_params=pltpu.CompilerParams(
            collective_id=0, has_side_effects=True, vmem_limit_bytes=32 * 1024 * 1024
        ),
        name="routed_backward",
    )(*[pltpu.with_memory_space_constraint(a, pltpu.HBM) for a in operands])


def solution(mesh):
    both = ("group", "member")
    return jax.shard_map(
        functools.partial(shards, mesh),
        mesh=mesh,
        in_specs=(
            P(both, None),
            P(both, None),
            P("group", None, None, None),
            P("group", None, None),
            P("group", None, None, None),
            P(both, None, None),
            P(both, None, None),
            P(both, None, None),
        ),
        out_specs=(
            P(both, None),
            P(both, None, None),
            P(both, None, None),
            P(both, None, None),
        ),
        check_vma=False,
    )
```

```python
import functools

import jax
import jax.numpy as jnp
from jax import lax
from jax.experimental import pallas as pl
from jax.experimental.pallas import tpu as pltpu
from jax.sharding import PartitionSpec as P

MESH = pl.DeviceIdType.MESH
CLASSES = 4
LANES = 128
F32 = jnp.float32
BF16 = jnp.bfloat16


def dot_nn(a, b):
    return jnp.dot(a, b, preferred_element_type=F32)


def dot_nt(a, b):
    return lax.dot_general(a, b, (((1,), (1,)), ((), ())), preferred_element_type=F32)


def far_first(n):
    return sorted(range(1, n), key=lambda o: -min(o, n - o))


def kernel(
    dims,
    x_hbm, dy_hbm, tok_hbm, cnt_hbm, prob_hbm, wg, wu, wd,
    gt_ref, gg, gu, gd,
    x_ref, dy_ref, tok_ref, cnt_ref, prob_ref,
    send_a, recv_a, t_all, z_send, rows, w_gu, w_dd, w_sib, acc_gu, acc_dh,
    d_pair, d_t, h_t, p_buf, snd, rcv, r2_send, r2_recv, r3_send, r3_recv,
    r4_send, r4_recv,
    in_sem, w_sem, small_send, small_recv, ring_send, ring_recv, sib_send, sib_recv,
    red_send, red_recv,
):
    ng, ny, nx, hs, cap, cw = dims
    nk = 2 * nx
    ns = ng * cap
    tg = ny * nk
    half = ns // 2
    span = ng // 2
    units = cw // LANES
    cut = -(-units // 2) * LANES
    parts = (pl.ds(0, cut), pl.ds(cut, cw - cut))
    pieces = [
        [slice(o, min(o + 256, hi)) for o in range(lo, hi, 256)]
        for lo, hi in ((0, cut), (cut, cw))
    ]

    z = lax.axis_index("group")
    m = lax.axis_index("member")
    y = m // nk
    k = m % nk
    x = k // 2
    c = k % 2
    brings = x % CLASSES
    own = k % CLASSES
    other = (own + 2) % CLASSES
    sibling = (z, y * nk + 2 * x + (1 - c))

    def along(steps):
        return (z, y * nk + 2 * ((x + steps + nx) % nx) + c)

    neighbour = (along(1), along(-1))

    def remote(src, dst, send_sem, recv_sem, device):
        return pltpu.make_async_remote_copy(
            src_ref=src, dst_ref=dst, send_sem=send_sem, recv_sem=recv_sem,
            device_id=device, device_id_type=MESH,
        )

    def arrived(ref, sem):
        pltpu.make_async_copy(ref, ref, sem).wait()

    def signal(device):
        pl.semaphore_signal(
            pltpu.get_barrier_semaphore(), inc=1, device_id=device, device_id_type=MESH
        )

    A, W, X, R4, B, C, R2, R3 = 0, 1, 2, 3, 4, 6, 8, 10

    for o in far_first(nk):
        signal((z, y * nk + (k + o) % nk))
    for o in far_first(ny):
        signal((z, ((y + o) % ny) * nk + k))
    for o in far_first(ng):
        signal(((z + o) % ng, m))

    inputs = [
        pltpu.make_async_copy(src, dst, in_sem.at[i])
        for i, (src, dst) in enumerate(
            (
                (x_hbm, x_ref), (dy_hbm, dy_ref), (tok_hbm, tok_ref), (cnt_hbm, cnt_ref),
                (prob_hbm, prob_ref),
            )
        )
    ]
    for copy in inputs:
        copy.start()
    loads = [
        pltpu.make_async_copy(wg.at[0], w_gu.at[pl.ds(0, hs)], w_sem.at[0]),
        pltpu.make_async_copy(wu.at[0], w_gu.at[pl.ds(hs, hs)], w_sem.at[1]),
        pltpu.make_async_copy(wd.at[0], w_dd.at[pl.ds(0, hs)], w_sem.at[2]),
        pltpu.make_async_copy(wd.at[0], w_dd.at[pl.ds(hs, hs)], w_sem.at[3]),
    ]
    for load in loads:
        load.start()
    for copy in inputs:
        copy.wait()

    send_a[...] = jnp.zeros_like(send_a)
    for u in range(CLASSES * units):
        cols = slice(u * LANES, (u + 1) * LANES)
        send_a[u // units, pl.ds(u % units, 1), :] = x_ref[:, cols].astype(F32)
        send_a[CLASSES + u // units, pl.ds(u % units, 1), :] = dy_ref[:, cols].astype(F32)

    pl.semaphore_wait(pltpu.get_barrier_semaphore(), (nk - 1) + (ny - 1) + (ng - 1))

    for o in far_first(nk):
        kk = (k + o) % nk
        remote(
            send_a.at[(kk % 2) * CLASSES + kk // 2 % CLASSES], recv_a.at[k], small_send.at[A], small_recv.at[A],
            (z, y * nk + kk),
        ).start()
    recv_a[k] = send_a[c * CLASSES + brings]

    row = lax.broadcasted_iota(jnp.int32, (ns, cap), 0)
    lane = lax.broadcasted_iota(jnp.int32, (ns, cap), 1)

    def spread(ref):
        wide = jnp.concatenate(
            [
                jnp.broadcast_to(ref[0, i, pl.ds(y, 1), :].astype(F32), (cap, cap))
                for i in range(ng)
            ],
            axis=0,
        )
        return jnp.sum(jnp.where(lane == row % cap, wide, 0.0), axis=1, keepdims=True)

    counts = jnp.concatenate(
        [
            jnp.broadcast_to(cnt_ref[0, pl.ds(i, 1), :].astype(F32), (cap, ny))
            for i in range(ng)
        ],
        axis=0,
    )
    expert = lax.broadcasted_iota(jnp.int32, (ns, ny), 1)
    counts = jnp.sum(jnp.where(expert == y, counts, 0.0), axis=1, keepdims=True)
    slot_token = spread(tok_ref)
    position = (lax.broadcasted_iota(jnp.int32, (ns, 1), 0) % cap).astype(F32)
    live = jnp.where(position < counts, 1.0, 0.0)
    core = c.astype(F32)
    factor = spread(prob_ref) * live * core + (1.0 - core)
    token = lax.broadcasted_iota(jnp.int32, (ns, tg), 1).astype(F32)
    sel = jnp.where(token == slot_token, 1.0, 0.0)
    sel_t = (sel * live).T.astype(BF16)
    sel = sel.astype(BF16)

    for load in loads:
        load.wait()
    for i in range(2):
        cols = pl.ds(pl.multiple_of((2 * i + 1 - c) * cw, LANES), cw)
        remote(
            w_gu.at[:, cols], w_sib.at[i], small_send.at[W], small_recv.at[W], sibling
        ).start()

    acc_gu[...] = jnp.zeros_like(acc_gu)
    acc_dh[...] = jnp.zeros_like(acc_dh)

    arrived(recv_a.at[pl.ds(0, nk - 1)], small_recv.at[A])
    t_all[y] = jnp.concatenate([recv_a[:, u, :] for u in range(units)], axis=1).astype(BF16)
    for p, part in enumerate(parts):
        if p:
            arrived(t_all.at[pl.ds(0, ny - 1), :, parts[0]], small_send.at[B])
        for o in far_first(ny):
            block = t_all.at[y, :, part]
            remote(
                block, block, small_send.at[B + p], small_recv.at[B + p],
                (z, ((y + o) % ny) * nk + k),
            ).start()
    here = pl.ds(pl.multiple_of(z * cap, cap), cap)
    for p, part in enumerate(parts):
        arrived(t_all.at[pl.ds(0, ny - 1), :, part], small_recv.at[B + p])
        for piece in pieces[p]:
            width = piece.stop - piece.start
            picked = dot_nn(sel, t_all[:, :, piece].reshape(tg, width)) * factor
            z_send[:, :, piece] = picked.astype(BF16).reshape(ng, cap, width)
        if p:
            arrived(z_send.at[pl.ds(0, ng - 1), :, parts[0]], small_send.at[C])
        for o in far_first(ng):
            g = (z + o) % ng
            remote(
                z_send.at[g, :, part], rows.at[c, brings, here, part],
                small_send.at[C + p], small_recv.at[C + p], (g, m),
            ).start()
    rows[c, brings, here, :] = z_send[z]

    moves = ((1, 0), (-1, 0), (1, 1), (-1, 1), (2, 0), (-2, 1))
    goes_on = {0: 4, 3: 5}

    def source(steps):
        return (brings + CLASSES - steps) % CLASSES

    def pass_on(quarter, i):
        steps, p = moves[i]
        block = rows.at[c, quarter, :, parts[p]]
        remote(
            block, block, ring_send.at[i], ring_recv.at[i], along(1 if steps > 0 else -1)
        ).start()

    def share(quarter, p, i):
        block = rows.at[c, quarter, :, parts[p]]
        remote(block, block, sib_send.at[i], sib_recv.at[i], sibling).start()

    def accumulate(quarter):
        cols = pl.ds(pl.multiple_of(quarter * cw, LANES), cw)
        acc_gu[...] += dot_nt(rows[0, quarter], w_gu[:, cols])
        acc_dh[...] += dot_nt(rows[1, quarter], w_dd[:, cols])

    for p, part in enumerate(parts):
        arrived(rows.at[c, brings, pl.ds(0, ns - cap), part], small_recv.at[C + p])
        pass_on(brings, 2 * p)
        pass_on(brings, 2 * p + 1)
        share(brings, p, 6 + p)
    for i in range(6):
        steps, p = moves[i]
        arrived(rows.at[c, source(steps), :, parts[p]], ring_recv.at[i])
        if i in goes_on:
            pass_on(source(steps), goes_on[i])
        share(source(steps), p, i)
        if i == 1:
            for p in range(2):
                arrived(rows.at[1 - c, brings, :, parts[p]], sib_recv.at[6 + p])
            accumulate(brings)
        if i in (3, 5):
            for j in (0, 1, 2, 3) if i == 3 else (4, 5):
                steps, p = moves[j]
                arrived(rows.at[1 - c, source(steps), :, parts[p]], sib_recv.at[j])
                if j in (2, 3, 5):
                    accumulate(source(steps))

    both = acc_gu[...]
    turned = pltpu.roll(both, hs, 1)
    left = lax.broadcasted_iota(jnp.int32, (ns, 2 * hs), 1) < hs
    gate = jnp.where(left, both, turned)
    up = jnp.where(left, turned, both)
    sg = jax.nn.sigmoid(gate)
    active = gate * sg
    d_hidden = acc_dh[...]
    d_both = jnp.where(
        left, d_hidden * up * sg * (1.0 + gate * (1.0 - sg)), d_hidden * active
    )
    d_pair[c] = d_both.astype(BF16)
    exchange = remote(d_pair.at[c], d_pair.at[c], small_send.at[X], small_recv.at[X], sibling)
    exchange.start()
    d_t[...] = d_both.T.astype(BF16)
    h_t[...] = (active * up).T[0:hs, :].astype(BF16)

    def gradients(quarter):
        for piece in pieces[0] + pieces[1]:
            cols = slice(quarter * cw + piece.start, quarter * cw + piece.stop)
            pair = dot_nn(d_t[...], rows[0, quarter, :, piece]).astype(BF16)
            gg[0, :, cols] = pair[0:hs]
            gu[0, :, cols] = pair[hs:]
            gd[0, :, cols] = dot_nn(h_t[...], rows[1, quarter, :, piece]).astype(BF16)

    def partial(quarter, h, piece):
        lines = slice(h * half, (h + 1) * half)
        width = piece.stop - piece.start
        cols = pl.ds(pl.multiple_of(quarter * cw + piece.start, LANES), width)
        return dot_nn(d_pair[c, lines, :], w_gu[:, cols]) + dot_nn(
            d_pair[1 - c, lines, :], w_sib[quarter // 2, :, piece]
        )

    arrived(w_sib, small_recv.at[W])
    arrived(d_pair.at[0], small_recv.at[X])

    for p, part in enumerate(parts):
        for h in range(2):
            for piece in pieces[p]:
                snd[h, :, piece] = partial(other, h, piece).astype(BF16)
            remote(
                snd.at[h, :, part], rcv.at[h, :, part], red_send.at[p, h], red_recv.at[p, h],
                neighbour[h],
            ).start()
    for h in range(2):
        for piece in pieces[0] + pieces[1]:
            p_buf[h, :, piece] = partial(own, h, piece)
    gradients(0)

    for p, part in enumerate(parts):
        for h in range(2):
            arrived(rcv.at[h, :, part], red_recv.at[p, h])
            for piece in pieces[p]:
                value = p_buf[h, :, piece] + rcv[h, :, piece].astype(F32)
                r2_send[pl.ds(h * span, span), :, piece] = value.astype(BF16).reshape(
                    span, cap, piece.stop - piece.start
                )
        for o in far_first(ng):
            s = (z + o) % ng
            remote(
                r2_send.at[s, :, part], r2_recv.at[z, :, part], small_send.at[R2 + p],
                small_recv.at[R2 + p], (s, m),
            ).start()
    r2_recv[z] = r2_send[z]
    gradients(1)
    gradients(2)
    for p, part in enumerate(parts):
        arrived(r2_recv.at[pl.ds(0, ng - 1), :, part], small_recv.at[R2 + p])
        for piece in pieces[p]:
            width = piece.stop - piece.start
            summed = dot_nn(sel_t, r2_recv[:, :, piece].reshape(ns, width))
            r3_send[:, :, piece] = summed.astype(BF16).reshape(ny, nk, width)
        for o in far_first(ny):
            to = (y + o) % ny
            remote(
                r3_send.at[to, :, part], r3_recv.at[y, :, part], small_send.at[R3 + p],
                small_recv.at[R3 + p], (z, to * nk + k),
            ).start()
    r3_recv[y] = r3_send[y]
    gradients(3)
    r4_send[...] = jnp.zeros_like(r4_send)

    arrived(recv_a.at[pl.ds(0, nk - 1)], small_send.at[A])
    arrived(t_all.at[pl.ds(0, ny - 1), :, parts[1]], small_send.at[B + 1])
    arrived(z_send.at[pl.ds(0, ng - 1), :, parts[1]], small_send.at[C + 1])
    arrived(w_sib, small_send.at[W])
    for i, (steps, p) in enumerate(moves):
        arrived(rows.at[0, 0, :, parts[p]], ring_send.at[i])
        arrived(rows.at[0, 0, :, parts[p]], sib_send.at[i])
    for p, part in enumerate(parts):
        arrived(rows.at[0, 0, :, part], sib_send.at[6 + p])
    for h in range(2):
        for p, part in enumerate(parts):
            arrived(snd.at[h, :, part], red_send.at[p, h])
    exchange.wait_send()
    for p, part in enumerate(parts):
        arrived(r2_send.at[pl.ds(0, ng - 1), :, part], small_send.at[R2 + p])

    for p, part in enumerate(parts):
        arrived(r3_recv.at[pl.ds(0, ny - 1), :, part], small_recv.at[R3 + p])
        for u in range(p * cut // LANES, units if p else cut // LANES):
            cols = slice(u * LANES, (u + 1) * LANES)
            r4_send[:, u, :] = jnp.sum(r3_recv[:, :, cols].astype(F32), axis=0)
    for o in far_first(nk):
        to = (k + o) % nk
        remote(
            r4_send.at[to], r4_recv.at[k], small_send.at[R4], small_recv.at[R4],
            (z, y * nk + to),
        ).start()
    r4_recv[k] = r4_send[k]
    for p, part in enumerate(parts):
        arrived(r3_send.at[pl.ds(0, ny - 1), :, part], small_send.at[R3 + p])
    arrived(r4_recv.at[pl.ds(0, nk - 1)], small_recv.at[R4])
    for quarter in range(CLASSES):
        total = r4_recv[quarter]
        for k2 in range(quarter + CLASSES, nk, CLASSES):
            total = total + r4_recv[k2]
        for u in range(units):
            cols = slice((quarter * units + u) * LANES, (quarter * units + u + 1) * LANES)
            gt_ref[:, cols] = total[u : u + 1, :].astype(BF16)
    arrived(r4_send.at[pl.ds(0, nk - 1)], small_send.at[R4])


def shards(mesh, tokens, grad_out, route_token, route_count, route_prob, w_gate, w_up, w_down):
    ng = mesh.shape["group"]
    ny = route_token.shape[2]
    cap = route_token.shape[3]
    nk = mesh.shape["member"] // ny
    hs, features = w_gate.shape[1:]
    cw = features // CLASSES
    assert cw % LANES == 0 and nk % (2 * CLASSES) == 0
    ns, tg, half, units = ng * cap, ny * nk, ng * cap // 2, cw // LANES
    low = -(-units // 8) * 8
    vmem = pl.BlockSpec(memory_space=pltpu.VMEM)
    hbm = pl.BlockSpec(memory_space=pl.ANY)
    dma = pltpu.SemaphoreType.DMA
    grad_shape = jax.ShapeDtypeStruct((1, hs, features), BF16)
    operands = (tokens, grad_out, route_token, route_count, route_prob, w_gate, w_up, w_down)
    return pl.pallas_call(
        functools.partial(kernel, (ng, ny, nk // 2, hs, cap, cw)),
        out_shape=(
            jax.ShapeDtypeStruct((1, features), BF16),
            grad_shape,
            grad_shape,
            grad_shape,
        ),
        in_specs=[hbm] * 8,
        out_specs=(vmem,) * 4,
        scratch_shapes=[
            pltpu.VMEM((1, features), BF16),
            pltpu.VMEM((1, features), BF16),
            pltpu.VMEM(route_token.shape, jnp.int32),
            pltpu.VMEM(route_count.shape, jnp.int32),
            pltpu.VMEM(route_prob.shape, F32),
            pltpu.VMEM((2 * CLASSES, low, LANES), F32),
            pltpu.VMEM((nk, low, LANES), F32),
            pltpu.VMEM((ny, nk, cw), BF16),
            pltpu.VMEM((ng, cap, cw), BF16),
            pltpu.VMEM((2, CLASSES, ns, cw), BF16),
            pltpu.VMEM((2 * hs, features), BF16),
            pltpu.VMEM((2 * hs, features), BF16),
            pltpu.VMEM((2, 2 * hs, cw), BF16),
            pltpu.VMEM((ns, 2 * hs), F32),
            pltpu.VMEM((ns, 2 * hs), F32),
            pltpu.VMEM((2, ns, 2 * hs), BF16),
            pltpu.VMEM((2 * hs, ns), BF16),
            pltpu.VMEM((hs, ns), BF16),
            pltpu.VMEM((2, half, cw), F32),
            pltpu.VMEM((2, half, cw), BF16),
            pltpu.VMEM((2, half, cw), BF16),
            pltpu.VMEM((ng, cap, cw), BF16),
            pltpu.VMEM((ng, cap, cw), BF16),
            pltpu.VMEM((ny, nk, cw), BF16),
            pltpu.VMEM((ny, nk, cw), BF16),
            pltpu.VMEM((nk, low, LANES), F32),
            pltpu.VMEM((nk, low, LANES), F32),
            dma((5,)),
            dma((4,)),
            dma((12,)),
            dma((12,)),
            dma((6,)),
            dma((6,)),
            dma((8,)),
            dma((8,)),
            dma((2, 2)),
            dma((2, 2)),
        ],
        compiler_params=pltpu.CompilerParams(
            collective_id=0, has_side_effects=True, vmem_limit_bytes=32 * 1024 * 1024
        ),
        name="routed_backward",
    )(*[pltpu.with_memory_space_constraint(a, pltpu.HBM) for a in operands])


def solution(mesh):
    both = ("group", "member")
    return jax.shard_map(
        functools.partial(shards, mesh),
        mesh=mesh,
        in_specs=(
            P(both, None),
            P(both, None),
            P("group", None, None, None),
            P("group", None, None),
            P("group", None, None, None),
            P(both, None, None),
            P(both, None, None),
            P(both, None, None),
        ),
        out_specs=(
            P(both, None),
            P(both, None, None),
            P(both, None, None),
            P(both, None, None),
        ),
        check_vma=False,
    )
```

```python
import functools

import jax
import jax.numpy as jnp
from jax import lax
from jax.experimental import pallas as pl
from jax.experimental.pallas import tpu as pltpu
from jax.sharding import PartitionSpec as P

MESH = pl.DeviceIdType.MESH
CLASSES = 4
LANES = 128
F32 = jnp.float32
BF16 = jnp.bfloat16


def dot_nn(a, b):
    return jnp.dot(a, b, preferred_element_type=F32)


def dot_nt(a, b):
    return lax.dot_general(a, b, (((1,), (1,)), ((), ())), preferred_element_type=F32)


def far_first(n):
    return sorted(range(1, n), key=lambda o: -min(o, n - o))


def kernel(
    dims,
    x_hbm, dy_hbm, tok_hbm, cnt_hbm, prob_hbm, wg, wu, wd,
    gt_ref, gg, gu, gd,
    x_ref, dy_ref, tok_ref, cnt_ref, prob_ref,
    send_a, recv_a, t_all, z_send, rows, w_gu, w_dd, w_sib, acc_gu, acc_dh,
    d_pair, d_t, h_t, p_buf, snd, rcv, r2_send, r2_recv, r3_send, r3_recv,
    r4_send, r4_recv,
    in_sem, w_sem, small_send, small_recv, ring_send, ring_recv, sib_send, sib_recv,
    red_send, red_recv,
):
    ng, ny, nx, hs, cap, cw = dims
    nk = 2 * nx
    ns = ng * cap
    tg = ny * nk
    half = ns // 2
    span = ng // 2
    units = cw // LANES
    cut = max(units // 2, 1) * LANES
    parts = (pl.ds(0, cut), pl.ds(cut, cw - cut))
    pieces = [
        [slice(o, min(o + 256, hi)) for o in range(lo, hi, 256)]
        for lo, hi in ((0, cut), (cut, cw))
    ]

    z = lax.axis_index("group")
    m = lax.axis_index("member")
    y = m // nk
    k = m % nk
    x = k // 2
    c = k % 2
    brings = x % CLASSES
    own = k % CLASSES
    other = (own + 2) % CLASSES
    sibling = (z, y * nk + 2 * x + (1 - c))

    def along(steps):
        return (z, y * nk + 2 * ((x + steps + nx) % nx) + c)

    neighbour = (along(1), along(-1))

    def remote(src, dst, send_sem, recv_sem, device):
        return pltpu.make_async_remote_copy(
            src_ref=src, dst_ref=dst, send_sem=send_sem, recv_sem=recv_sem,
            device_id=device, device_id_type=MESH,
        )

    def arrived(ref, sem):
        pltpu.make_async_copy(ref, ref, sem).wait()

    def signal(device):
        pl.semaphore_signal(
            pltpu.get_barrier_semaphore(), inc=1, device_id=device, device_id_type=MESH
        )

    A, W, X, R4, B, C, R2, R3 = 0, 1, 2, 3, 4, 6, 8, 10

    for o in far_first(nk):
        signal((z, y * nk + (k + o) % nk))
    for o in far_first(ny):
        signal((z, ((y + o) % ny) * nk + k))
    for o in far_first(ng):
        signal(((z + o) % ng, m))

    inputs = [
        pltpu.make_async_copy(src, dst, in_sem.at[i])
        for i, (src, dst) in enumerate(
            (
                (x_hbm, x_ref), (dy_hbm, dy_ref), (tok_hbm, tok_ref), (cnt_hbm, cnt_ref),
                (prob_hbm, prob_ref),
            )
        )
    ]
    for copy in inputs:
        copy.start()
    loads = [
        pltpu.make_async_copy(wg.at[0], w_gu.at[pl.ds(0, hs)], w_sem.at[0]),
        pltpu.make_async_copy(wu.at[0], w_gu.at[pl.ds(hs, hs)], w_sem.at[1]),
        pltpu.make_async_copy(wd.at[0], w_dd.at[pl.ds(0, hs)], w_sem.at[2]),
        pltpu.make_async_copy(wd.at[0], w_dd.at[pl.ds(hs, hs)], w_sem.at[3]),
    ]
    for load in loads:
        load.start()
    for copy in inputs:
        copy.wait()

    send_a[...] = jnp.zeros_like(send_a)
    for u in range(CLASSES * units):
        cols = slice(u * LANES, (u + 1) * LANES)
        send_a[u // units, pl.ds(u % units, 1), :] = x_ref[:, cols].astype(F32)
        send_a[CLASSES + u // units, pl.ds(u % units, 1), :] = dy_ref[:, cols].astype(F32)

    pl.semaphore_wait(pltpu.get_barrier_semaphore(), (nk - 1) + (ny - 1) + (ng - 1))

    for o in far_first(nk):
        kk = (k + o) % nk
        remote(
            send_a.at[(kk % 2) * CLASSES + kk // 2 % CLASSES], recv_a.at[k], small_send.at[A], small_recv.at[A],
            (z, y * nk + kk),
        ).start()
    recv_a[k] = send_a[c * CLASSES + brings]

    row = lax.broadcasted_iota(jnp.int32, (ns, cap), 0)
    lane = lax.broadcasted_iota(jnp.int32, (ns, cap), 1)

    def spread(ref):
        wide = jnp.concatenate(
            [
                jnp.broadcast_to(ref[0, i, pl.ds(y, 1), :].astype(F32), (cap, cap))
                for i in range(ng)
            ],
            axis=0,
        )
        return jnp.sum(jnp.where(lane == row % cap, wide, 0.0), axis=1, keepdims=True)

    counts = jnp.concatenate(
        [
            jnp.broadcast_to(cnt_ref[0, pl.ds(i, 1), :].astype(F32), (cap, ny))
            for i in range(ng)
        ],
        axis=0,
    )
    expert = lax.broadcasted_iota(jnp.int32, (ns, ny), 1)
    counts = jnp.sum(jnp.where(expert == y, counts, 0.0), axis=1, keepdims=True)
    slot_token = spread(tok_ref)
    position = (lax.broadcasted_iota(jnp.int32, (ns, 1), 0) % cap).astype(F32)
    live = jnp.where(position < counts, 1.0, 0.0)
    core = c.astype(F32)
    factor = spread(prob_ref) * live * core + (1.0 - core)
    token = lax.broadcasted_iota(jnp.int32, (ns, tg), 1).astype(F32)
    sel = jnp.where(token == slot_token, 1.0, 0.0)
    sel_t = (sel * live).T.astype(BF16)
    sel = sel.astype(BF16)

    for load in loads:
        load.wait()
    for i in range(2):
        cols = pl.ds(pl.multiple_of((2 * i + 1 - c) * cw, LANES), cw)
        remote(
            w_gu.at[:, cols], w_sib.at[i], small_send.at[W], small_recv.at[W], sibling
        ).start()

    acc_gu[...] = jnp.zeros_like(acc_gu)
    acc_dh[...] = jnp.zeros_like(acc_dh)

    arrived(recv_a.at[pl.ds(0, nk - 1)], small_recv.at[A])
    t_all[y] = jnp.concatenate([recv_a[:, u, :] for u in range(units)], axis=1).astype(BF16)
    for p, part in enumerate(parts):
        for o in far_first(ny):
            block = t_all.at[y, :, part]
            remote(
                block, block, small_send.at[B + p], small_recv.at[B + p],
                (z, ((y + o) % ny) * nk + k),
            ).start()
    here = pl.ds(pl.multiple_of(z * cap, cap), cap)
    for p, part in enumerate(parts):
        arrived(t_all.at[pl.ds(0, ny - 1), :, part], small_recv.at[B + p])
        for piece in pieces[p]:
            width = piece.stop - piece.start
            picked = dot_nn(sel, t_all[:, :, piece].reshape(tg, width)) * factor
            z_send[:, :, piece] = picked.astype(BF16).reshape(ng, cap, width)
        for o in far_first(ng):
            g = (z + o) % ng
            remote(
                z_send.at[g, :, part], rows.at[c, brings, here, part],
                small_send.at[C + p], small_recv.at[C + p], (g, m),
            ).start()
    rows[c, brings, here, :] = z_send[z]

    moves = ((1, 0), (-1, 0), (1, 1), (-1, 1), (2, 0), (-2, 1))
    goes_on = {0: 4, 3: 5}

    def source(steps):
        return (brings + CLASSES - steps) % CLASSES

    def pass_on(quarter, i):
        steps, p = moves[i]
        block = rows.at[c, quarter, :, parts[p]]
        remote(
            block, block, ring_send.at[i], ring_recv.at[i], along(1 if steps > 0 else -1)
        ).start()

    def share(quarter, p, i):
        block = rows.at[c, quarter, :, parts[p]]
        remote(block, block, sib_send.at[i], sib_recv.at[i], sibling).start()

    def accumulate(quarter):
        cols = pl.ds(pl.multiple_of(quarter * cw, LANES), cw)
        acc_gu[...] += dot_nt(rows[0, quarter], w_gu[:, cols])
        acc_dh[...] += dot_nt(rows[1, quarter], w_dd[:, cols])

    for p, part in enumerate(parts):
        arrived(rows.at[c, brings, pl.ds(0, ns - cap), part], small_recv.at[C + p])
        pass_on(brings, 2 * p)
        pass_on(brings, 2 * p + 1)
        share(brings, p, 6 + p)
    for i in range(6):
        steps, p = moves[i]
        arrived(rows.at[c, source(steps), :, parts[p]], ring_recv.at[i])
        if i in goes_on:
            pass_on(source(steps), goes_on[i])
        share(source(steps), p, i)
        if i == 1:
            for p in range(2):
                arrived(rows.at[1 - c, brings, :, parts[p]], sib_recv.at[6 + p])
            accumulate(brings)
        if i in (3, 5):
            for j in (0, 1, 2, 3) if i == 3 else (4, 5):
                steps, p = moves[j]
                arrived(rows.at[1 - c, source(steps), :, parts[p]], sib_recv.at[j])
                if j in (2, 3, 5):
                    accumulate(source(steps))

    both = acc_gu[...]
    turned = pltpu.roll(both, hs, 1)
    left = lax.broadcasted_iota(jnp.int32, (ns, 2 * hs), 1) < hs
    gate = jnp.where(left, both, turned)
    up = jnp.where(left, turned, both)
    sg = jax.nn.sigmoid(gate)
    active = gate * sg
    d_hidden = acc_dh[...]
    d_both = jnp.where(
        left, d_hidden * up * sg * (1.0 + gate * (1.0 - sg)), d_hidden * active
    )
    d_pair[c] = d_both.astype(BF16)
    exchange = remote(d_pair.at[c], d_pair.at[c], small_send.at[X], small_recv.at[X], sibling)
    exchange.start()
    d_t[...] = d_both.T.astype(BF16)
    h_t[...] = (active * up).T[0:hs, :].astype(BF16)

    def gradients(quarter):
        for piece in pieces[0] + pieces[1]:
            cols = slice(quarter * cw + piece.start, quarter * cw + piece.stop)
            pair = dot_nn(d_t[...], rows[0, quarter, :, piece]).astype(BF16)
            gg[0, :, cols] = pair[0:hs]
            gu[0, :, cols] = pair[hs:]
            gd[0, :, cols] = dot_nn(h_t[...], rows[1, quarter, :, piece]).astype(BF16)

    def partial(quarter, h, piece):
        lines = slice(h * half, (h + 1) * half)
        width = piece.stop - piece.start
        cols = pl.ds(pl.multiple_of(quarter * cw + piece.start, LANES), width)
        return dot_nn(d_pair[c, lines, :], w_gu[:, cols]) + dot_nn(
            d_pair[1 - c, lines, :], w_sib[quarter // 2, :, piece]
        )

    arrived(w_sib, small_recv.at[W])
    arrived(d_pair.at[0], small_recv.at[X])

    for p, part in enumerate(parts):
        for h in range(2):
            for piece in pieces[p]:
                snd[h, :, piece] = partial(other, h, piece).astype(BF16)
            remote(
                snd.at[h, :, part], rcv.at[h, :, part], red_send.at[p, h], red_recv.at[p, h],
                neighbour[h],
            ).start()
    for h in range(2):
        for piece in pieces[0] + pieces[1]:
            p_buf[h, :, piece] = partial(own, h, piece)
    gradients(0)

    for p, part in enumerate(parts):
        for h in range(2):
            arrived(rcv.at[h, :, part], red_recv.at[p, h])
            for piece in pieces[p]:
                value = p_buf[h, :, piece] + rcv[h, :, piece].astype(F32)
                r2_send[pl.ds(h * span, span), :, piece] = value.astype(BF16).reshape(
                    span, cap, piece.stop - piece.start
                )
        for o in far_first(ng):
            s = (z + o) % ng
            remote(
                r2_send.at[s, :, part], r2_recv.at[z, :, part], small_send.at[R2 + p],
                small_recv.at[R2 + p], (s, m),
            ).start()
    r2_recv[z] = r2_send[z]
    gradients(1)
    gradients(2)
    for p, part in enumerate(parts):
        arrived(r2_recv.at[pl.ds(0, ng - 1), :, part], small_recv.at[R2 + p])
        for piece in pieces[p]:
            width = piece.stop - piece.start
            summed = dot_nn(sel_t, r2_recv[:, :, piece].reshape(ns, width))
            r3_send[:, :, piece] = summed.astype(BF16).reshape(ny, nk, width)
        for o in far_first(ny):
            to = (y + o) % ny
            remote(
                r3_send.at[to, :, part], r3_recv.at[y, :, part], small_send.at[R3 + p],
                small_recv.at[R3 + p], (z, to * nk + k),
            ).start()
    r3_recv[y] = r3_send[y]
    gradients(3)
    r4_send[...] = jnp.zeros_like(r4_send)

    arrived(recv_a.at[pl.ds(0, nk - 1)], small_send.at[A])
    for p, part in enumerate(parts):
        arrived(t_all.at[pl.ds(0, ny - 1), :, part], small_send.at[B + p])
    for p, part in enumerate(parts):
        arrived(z_send.at[pl.ds(0, ng - 1), :, part], small_send.at[C + p])
    arrived(w_sib, small_send.at[W])
    for i, (steps, p) in enumerate(moves):
        arrived(rows.at[0, 0, :, parts[p]], ring_send.at[i])
        arrived(rows.at[0, 0, :, parts[p]], sib_send.at[i])
    for p, part in enumerate(parts):
        arrived(rows.at[0, 0, :, part], sib_send.at[6 + p])
    for h in range(2):
        for p, part in enumerate(parts):
            arrived(snd.at[h, :, part], red_send.at[p, h])
    exchange.wait_send()
    for p, part in enumerate(parts):
        arrived(r2_send.at[pl.ds(0, ng - 1), :, part], small_send.at[R2 + p])

    for p, part in enumerate(parts):
        arrived(r3_recv.at[pl.ds(0, ny - 1), :, part], small_recv.at[R3 + p])
        for u in range(p * cut // LANES, units if p else cut // LANES):
            cols = slice(u * LANES, (u + 1) * LANES)
            r4_send[:, u, :] = jnp.sum(r3_recv[:, :, cols].astype(F32), axis=0)
    for o in far_first(nk):
        to = (k + o) % nk
        remote(
            r4_send.at[to], r4_recv.at[k], small_send.at[R4], small_recv.at[R4],
            (z, y * nk + to),
        ).start()
    r4_recv[k] = r4_send[k]
    for p, part in enumerate(parts):
        arrived(r3_send.at[pl.ds(0, ny - 1), :, part], small_send.at[R3 + p])
    arrived(r4_recv.at[pl.ds(0, nk - 1)], small_recv.at[R4])
    for quarter in range(CLASSES):
        total = r4_recv[quarter]
        for k2 in range(quarter + CLASSES, nk, CLASSES):
            total = total + r4_recv[k2]
        for u in range(units):
            cols = slice((quarter * units + u) * LANES, (quarter * units + u + 1) * LANES)
            gt_ref[:, cols] = total[u : u + 1, :].astype(BF16)
    arrived(r4_send.at[pl.ds(0, nk - 1)], small_send.at[R4])


def shards(mesh, tokens, grad_out, route_token, route_count, route_prob, w_gate, w_up, w_down):
    ng = mesh.shape["group"]
    ny = route_token.shape[2]
    cap = route_token.shape[3]
    nk = mesh.shape["member"] // ny
    hs, features = w_gate.shape[1:]
    cw = features // CLASSES
    assert cw % LANES == 0 and nk % (2 * CLASSES) == 0
    ns, tg, half, units = ng * cap, ny * nk, ng * cap // 2, cw // LANES
    low = -(-units // 8) * 8
    vmem = pl.BlockSpec(memory_space=pltpu.VMEM)
    hbm = pl.BlockSpec(memory_space=pl.ANY)
    dma = pltpu.SemaphoreType.DMA
    grad_shape = jax.ShapeDtypeStruct((1, hs, features), BF16)
    operands = (tokens, grad_out, route_token, route_count, route_prob, w_gate, w_up, w_down)
    return pl.pallas_call(
        functools.partial(kernel, (ng, ny, nk // 2, hs, cap, cw)),
        out_shape=(
            jax.ShapeDtypeStruct((1, features), BF16),
            grad_shape,
            grad_shape,
            grad_shape,
        ),
        in_specs=[hbm] * 8,
        out_specs=(vmem,) * 4,
        scratch_shapes=[
            pltpu.VMEM((1, features), BF16),
            pltpu.VMEM((1, features), BF16),
            pltpu.VMEM(route_token.shape, jnp.int32),
            pltpu.VMEM(route_count.shape, jnp.int32),
            pltpu.VMEM(route_prob.shape, F32),
            pltpu.VMEM((2 * CLASSES, low, LANES), F32),
            pltpu.VMEM((nk, low, LANES), F32),
            pltpu.VMEM((ny, nk, cw), BF16),
            pltpu.VMEM((ng, cap, cw), BF16),
            pltpu.VMEM((2, CLASSES, ns, cw), BF16),
            pltpu.VMEM((2 * hs, features), BF16),
            pltpu.VMEM((2 * hs, features), BF16),
            pltpu.VMEM((2, 2 * hs, cw), BF16),
            pltpu.VMEM((ns, 2 * hs), F32),
            pltpu.VMEM((ns, 2 * hs), F32),
            pltpu.VMEM((2, ns, 2 * hs), BF16),
            pltpu.VMEM((2 * hs, ns), BF16),
            pltpu.VMEM((hs, ns), BF16),
            pltpu.VMEM((2, half, cw), F32),
            pltpu.VMEM((2, half, cw), BF16),
            pltpu.VMEM((2, half, cw), BF16),
            pltpu.VMEM((ng, cap, cw), BF16),
            pltpu.VMEM((ng, cap, cw), BF16),
            pltpu.VMEM((ny, nk, cw), BF16),
            pltpu.VMEM((ny, nk, cw), BF16),
            pltpu.VMEM((nk, low, LANES), F32),
            pltpu.VMEM((nk, low, LANES), F32),
            dma((5,)),
            dma((4,)),
            dma((12,)),
            dma((12,)),
            dma((6,)),
            dma((6,)),
            dma((8,)),
            dma((8,)),
            dma((2, 2)),
            dma((2, 2)),
        ],
        compiler_params=pltpu.CompilerParams(
            collective_id=0, has_side_effects=True, vmem_limit_bytes=32 * 1024 * 1024
        ),
        name="routed_backward",
    )(*[pltpu.with_memory_space_constraint(a, pltpu.HBM) for a in operands])


def solution(mesh):
    both = ("group", "member")
    return jax.shard_map(
        functools.partial(shards, mesh),
        mesh=mesh,
        in_specs=(
            P(both, None),
            P(both, None),
            P("group", None, None, None),
            P("group", None, None),
            P("group", None, None, None),
            P(both, None, None),
            P(both, None, None),
            P(both, None, None),
        ),
        out_specs=(
            P(both, None),
            P(both, None, None),
            P(both, None, None),
            P(both, None, None),
        ),
        check_vma=False,
    )
```
